32 devices in a mesh: shot: 4 (over y, core), dom: 8 (over z, x).
Axes of the slice: x: 2, y: 2, z: 4, core: 2. Of those that a mesh axis runs over, the one named last changes fastest.
Arguments:
- wave_before: float32 [4, 128, 64, 256], P('shot', 'dom'), may hold values from -1.5 to 1.5
- wave_current: float32 [4, 128, 64, 256], P('shot', 'dom'), may hold values from -1.5 to 1.5
- adjoint_far: float32 [4, 128, 64, 256], P('shot', 'dom'), may hold values from -1.5 to 1.5
- adjoint_near: float32 [4, 128, 64, 256], P('shot', 'dom'), may hold values from -1.5 to 1.5
- labels: int32 [128, 64, 256], P('dom'), may hold values from 0 to 7
- table: float32 [8], replicated, may hold values from 0.03 to 0.12
- source_index: int32 [4, 3], P('shot'), may hold values from 0 to 255, as said below
- wavelet: float32 [4, 4], P('shot'), may hold values from -6 to 6
- receiver_index: int32 [4, 1024, 3], P('shot'), may hold values from 0 to 255, as said below
- residual: float32 [4, 4, 1024], P('shot'), may hold values from -6 to 6
Outputs:
- final_wave: float32 [4, 128, 64, 256], P('shot', 'dom')
- first_adjoint: float32 [4, 128, 64, 256], P('shot', 'dom')
- gradient: float32 [128, 64, 256], P('dom')
The draws below stay inside these ranges and needn't reach their ends.
Inputs may be any that keep to these rules, and one draw needn't show every extreme that they name: `source_index`: column 0 is a cell index along x below 128, column 1 along z below 64, column 2 along y below 256. The first shot's source lies at the far corner of the grid and the second shot's source at depth 0. `receiver_index`: last index 0 is a cell index along x below 128, 1 along z below 64, 2 along y below 256; receivers may share a cell. In every shot the first receiver lies at the far corner of the grid and the second at depth 0.
All inputs are finite; a program needn't handle non-finite values.
Results may differ from the reference program's by a relative error of at most 0.00002.
Values sent between devices are 32-bit elements; how exact they have to be, the bound alone decides.
No kernel may reach another device: no remote copies, remote signals or barrier semaphores. Data moves between devices by JAX's collectives and lax.ppermute only.
A program may use at most 128 MiB of HBM per device.

```python
import math
import jax
import jax.numpy as jnp
from jax import lax

NZ = 64
NY = 256
RECS = 1024
STEPS = 4
REGIONS = 8
SHOTS = 4
NX = 128


def draw_source_index(key, part):
    keys = jax.random.split(jax.random.fold_in(key, 11), 3)
    along_x = jax.random.randint(keys[0], (SHOTS,), 0, NX)
    along_z = jax.random.randint(keys[1], (SHOTS,), 0, NZ)
    along_y = jax.random.randint(keys[2], (SHOTS,), 0, NY)
    along_x = along_x.at[0].set(NX - 1)
    along_z = along_z.at[0].set(NZ - 1)
    along_y = along_y.at[0].set(NY - 1)
    along_z = along_z.at[1].set(0)
    return jnp.stack([along_x, along_z, along_y], axis=-1).astype(jnp.int32)


def draw_receiver_index(key, part):
    keys = jax.random.split(jax.random.fold_in(key, 23), 3)
    along_x = jax.random.randint(keys[0], (SHOTS, RECS), 0, NX)
    along_z = jax.random.randint(keys[1], (SHOTS, RECS), 0, NZ)
    along_y = jax.random.randint(keys[2], (SHOTS, RECS), 0, NY)
    along_x = along_x.at[:, 0].set(NX - 1)
    along_z = along_z.at[:, 0].set(NZ - 1)
    along_y = along_y.at[:, 0].set(NY - 1)
    along_z = along_z.at[:, 1].set(0)
    return jnp.stack([along_x, along_z, along_y], axis=-1).astype(jnp.int32)


def plant(values, key, smallest, top_value):
    dims = values.shape
    index_at = [jax.random.randint(jax.random.fold_in(key, axis), (), 0, dims[axis]) for axis in range(len(dims))]
    values = values.at[tuple(index_at)].set(smallest)
    longest = dims.index(max(dims))
    index_at[longest] = (index_at[longest] + 1) % dims[longest]
    return values.at[tuple(index_at)].set(top_value)


def shard_levels(rng, extent, shards, low, high):
    def one(dim, shards_of):
        heights = jax.random.uniform(jax.random.fold_in(jax.random.fold_in(rng, 6), dim), (shards_of,), jnp.float32, low / len(shards), high / len(shards))
        return jnp.repeat(jnp.exp(heights), extent[dim] // shards_of).reshape((-1,) + (1,) * (len(extent) - dim - 1))

    level = one(*shards[0])
    for cut in shards[1:]:
        level = level * one(*cut)
    return level


def scatter_about(key, dims, deviation, bound, cuts=(), dtype=jnp.bfloat16):
    entries = deviation * jax.random.normal(key, dims, jnp.float32)
    if cuts:
        entries = entries * shard_levels(key, dims, cuts, -0.22, 0.18)
    return jnp.clip(entries, -bound, bound).astype(dtype)


def setup_inputs(seed: int = 0) -> dict:
    seeds = jax.random.split(jax.random.key(seed), 11)
    wave_before = scatter_about(seeds[0], (SHOTS, NX, NZ, NY), 0.25, 1.5, ((0, 4), (1, 8)), jnp.float32)
    wave_current = scatter_about(seeds[1], (SHOTS, NX, NZ, NY), 0.25, 1.5, ((0, 4), (1, 8)), jnp.float32)
    adjoint_far = scatter_about(seeds[2], (SHOTS, NX, NZ, NY), 0.25, 1.5, ((0, 4), (1, 8)), jnp.float32)
    adjoint_near = scatter_about(seeds[3], (SHOTS, NX, NZ, NY), 0.25, 1.5, ((0, 4), (1, 8)), jnp.float32)
    labels = plant(jax.random.randint(seeds[4], (NX, NZ, NY), 0, REGIONS), jax.random.fold_in(seeds[4], 1), 0, REGIONS - 1).astype(jnp.int32)
    table = jnp.clip(jnp.exp(jax.random.uniform(seeds[5], (REGIONS,), jnp.float32, math.log(0.03), math.log(0.12))), 0.03, 0.12)
    source_index = draw_source_index(jax.random.fold_in(seeds[10], 71), 0)
    wavelet = scatter_about(seeds[7], (SHOTS, STEPS), 1.0, 6.0, ((0, 4),), jnp.float32)
    receiver_index = draw_receiver_index(jax.random.fold_in(seeds[10], 71), 0)
    residual = scatter_about(seeds[9], (SHOTS, STEPS, RECS), 1.0, 6.0, ((0, 4),), jnp.float32)
    return dict(wave_before=wave_before, wave_current=wave_current, adjoint_far=adjoint_far, adjoint_near=adjoint_near, labels=labels, table=table, source_index=source_index, wavelet=wavelet, receiver_index=receiver_index, residual=residual)


centre_coef = -205.0 / 72.0
side_coefs = (8.0 / 5.0, -1.0 / 5.0, 8.0 / 315.0, -1.0 / 560.0)


def laplace(field_in):
    size_x, size_z, size_y = field_in.shape
    padded = jnp.pad(field_in, 4)
    result = 3.0 * centre_coef * field_in
    for k in range(1, 5):
        coef = side_coefs[k - 1]
        result = result + coef * (
            padded[4 + k:4 + k + size_x, 4:4 + size_z, 4:4 + size_y]
            + padded[4 - k:4 - k + size_x, 4:4 + size_z, 4:4 + size_y]
            + padded[4:4 + size_x, 4 + k:4 + k + size_z, 4:4 + size_y]
            + padded[4:4 + size_x, 4 - k:4 - k + size_z, 4:4 + size_y]
            + padded[4:4 + size_x, 4:4 + size_z, 4 + k:4 + k + size_y]
            + padded[4:4 + size_x, 4:4 + size_z, 4 - k:4 - k + size_y])
    return result


def rates(labels, table):
    result = jnp.zeros(labels.shape, jnp.float32)
    for region in range(REGIONS):
        result = result + jnp.where(labels == region, table[region], jnp.zeros((), jnp.float32))
    return result


def one_shot(rate, items):
    wave_old, wave_now, far_field, near_field, source, wave_amps, receivers, traces = items
    previous, current = wave_old, wave_now
    stored = []
    for step in range(STEPS):
        lap_current = laplace(current)
        stored.append(lap_current)
        upcoming = 2.0 * current - previous + rate * lap_current
        upcoming = upcoming.at[source[0], source[1], source[2]].add(wave_amps[step])
        previous, current = current, upcoming
    later, adjoint = far_field, near_field
    gradient = jnp.zeros_like(rate)
    for step in reversed(range(STEPS)):
        gradient = gradient + adjoint * stored[step]
        earlier = 2.0 * adjoint - later + laplace(rate * adjoint)
        earlier = earlier.at[receivers[:, 0], receivers[:, 1], receivers[:, 2]].add(traces[step])
        later, adjoint = adjoint, earlier
    return current, adjoint, gradient


def reference(wave_before, wave_current, adjoint_far, adjoint_near, labels, table, source_index, wavelet, receiver_index, residual):
    rate = rates(labels, table)
    final_wave, first_adjoint, gradients = lax.map(
        lambda items: one_shot(rate, items),
        (wave_before, wave_current, adjoint_far, adjoint_near, source_index, wavelet, receiver_index, residual))
    return final_wave, first_adjoint, jnp.sum(gradients, axis=0)
```

```python
import functools

import jax
import jax.numpy as jnp
from jax import lax
from jax.experimental import pallas as pl
from jax.experimental.pallas import tpu as pltpu
from jax.sharding import PartitionSpec as P

centre_coef = -205.0 / 72.0
side_coefs = (8.0 / 5.0, -1.0 / 5.0, 8.0 / 315.0, -1.0 / 560.0)
unit = 5040.0
side_units = (8064.0, -1008.0, 128.0, -9.0)
halo = 4

vmem = pl.BlockSpec(memory_space=pltpu.VMEM)
smem = pl.BlockSpec(memory_space=pltpu.SMEM)


def call(kernel, args, in_specs, out_shapes, scratch=(), flops=0):
    moved = sum(a.size * a.dtype.itemsize for a in args) + sum(4 * s.size for s in out_shapes)
    return pl.pallas_call(
        kernel,
        out_shape=out_shapes,
        in_specs=in_specs,
        out_specs=[vmem] * len(out_shapes),
        scratch_shapes=list(scratch),
        compiler_params=pltpu.CompilerParams(vmem_limit_bytes=24 * 1024 * 1024),
        cost_estimate=pl.CostEstimate(flops=flops, bytes_accessed=moved, transcendentals=0),
    )(*args)


def f32(*shape):
    return jax.ShapeDtypeStruct(shape, jnp.float32)


def band(size, block):
    row = lax.broadcasted_iota(jnp.int32, (size, size), 0)
    col = lax.broadcasted_iota(jnp.int32, (size, size), 1)
    apart = jnp.abs(row - col)
    value = jnp.zeros((size, size), jnp.float32)
    for k in range(1, 5):
        value = jnp.where(apart == k, side_units[k - 1], value)
    if block != size:
        value = jnp.where(lax.div(row, block) == lax.div(col, block), value, 0.0)
    return value.astype(jnp.bfloat16)


def pieces(value):
    high = value.astype(jnp.bfloat16)
    rest = value - high.astype(jnp.float32)
    middle = rest.astype(jnp.bfloat16)
    low = (rest - middle.astype(jnp.float32)).astype(jnp.bfloat16)
    return high, middle, low


def dot(a, b):
    return lax.dot_general(a, b, (((1,), (0,)), ((), ())), preferred_element_type=jnp.float32)


def laplacian(ext, first, group, along_y, along_z):
    _, nz, ny = ext.shape
    centre = ext[pl.ds(first + halo, group)]
    high, middle, low = pieces(centre.reshape(group * nz, ny))
    across = dot(low, along_y) + dot(along_z, low)
    across = across + (dot(middle, along_y) + dot(along_z, middle))
    across = across + (dot(high, along_y) + dot(along_z, high))
    result = 3.0 * centre_coef * centre + across.reshape(group, nz, ny) * (1.0 / unit)
    for k in range(1, 5):
        result = result + side_coefs[k - 1] * (
            ext[pl.ds(first + halo + k, group)] + ext[pl.ds(first + halo - k, group)]
        )
    return result


def group_of(planes, nz):
    group = max(1, min(planes, 256 // nz))
    while planes % group:
        group -= 1
    return group


def place(ext, info, near, far):
    planes = ext.shape[0] - 2 * halo
    odd = info[0]
    spot = jnp.where(odd == 1, 0, planes + halo)
    ext[pl.ds(spot, halo)] = near[...]
    ext[pl.ds(planes + halo - spot, halo)] = far[...]


def edge_spots(info, planes):
    odd = info[0]
    near = jnp.where(odd == 1, 0, planes - halo)
    return near, planes - halo - near


def prepare_kernel(info, table, labels, field, rate, near_edge, far_edge):
    value = jnp.zeros(labels.shape, jnp.float32)
    label = labels[...]
    for region in range(table.shape[0]):
        value = jnp.where(label == region, table[region], value)
    rate[...] = value
    near, far = edge_spots(info, labels.shape[0])
    near_edge[...] = rate[pl.ds(near, halo)] * field[pl.ds(near, halo)]
    far_edge[...] = rate[pl.ds(far, halo)] * field[pl.ds(far, halo)]


def receivers_kernel(info, index, values, injected):
    steps, planes, nz, ny = injected.shape
    count = index.shape[1]
    local = index[0:1, :] - info[1]
    cell = jnp.where((local >= 0) & (local < planes), local * nz + index[1:2, :], -1)
    at_y = lax.broadcasted_iota(jnp.int32, (ny, count), 0) == index[2:3, :]
    parts = []
    for step in range(steps):
        for piece in pieces(values[step : step + 1, :]):
            spread = jnp.where(at_y, piece.astype(jnp.float32), 0.0)
            parts.append(spread.astype(jnp.bfloat16))
    group = group_of(planes, nz)
    rows = group * nz
    for part in range(planes // group):
        at_cell = lax.broadcasted_iota(jnp.int32, (rows, count), 0) + part * rows == cell
        picked = jnp.where(at_cell, 1.0, 0.0).astype(jnp.bfloat16)
        for step in range(steps):
            total = None
            for piece in reversed(parts[3 * step : 3 * step + 3]):
                term = lax.dot_general(
                    picked, piece, (((1,), (1,)), ((), ())), preferred_element_type=jnp.float32
                )
                total = term if total is None else total + term
            injected[step, pl.ds(part * group, group)] = total.reshape(group, nz, ny)


def forward_kernel(step, with_edges, info, source, wavelet, *refs):
    if with_edges:
        current, previous, near, far, rate, upcoming, lap, near_edge, far_edge, ext = refs
    else:
        current, previous, near, far, rate, partial, adjoint, upcoming, keep, send, ext = refs
    planes, nz, ny = current.shape
    place(ext, info, near, far)
    ext[pl.ds(halo, planes)] = current[...]
    group = group_of(planes, nz)
    along_y = band(ny, ny)
    along_z = band(group * nz, nz)
    half = planes // 2
    for part in range(planes // group):
        first = part * group
        here = pl.ds(first, group)
        value = laplacian(ext, first, group, along_y, along_z)
        upcoming[here] = 2.0 * current[here] - previous[here] + rate[here] * value
        if with_edges:
            lap[here] = value
        else:
            ext[here] = partial[here] + adjoint[here] * value
    x = source[0, 0] - info[1]
    z = source[0, 1]
    y = source[0, 2]

    @pl.when((x >= 0) & (x < planes))
    def _():
        base = pl.multiple_of(lax.div(z, 8) * 8, 8)
        rows = lax.broadcasted_iota(jnp.int32, (8, ny), 0)
        cols = lax.broadcasted_iota(jnp.int32, (8, ny), 1)
        hit = (rows == z - base) & (cols == y)
        tile = upcoming[x, pl.ds(base, 8), :]
        upcoming[x, pl.ds(base, 8), :] = tile + jnp.where(hit, wavelet[0, step], 0.0)

    if with_edges:
        near_at, far_at = edge_spots(info, planes)
        near_edge[...] = upcoming[pl.ds(near_at, halo)]
        far_edge[...] = upcoming[pl.ds(far_at, halo)]
    else:
        mine = info[2] * half
        keep[...] = ext[pl.ds(mine, half)]
        send[...] = ext[pl.ds(half - mine, half)]


def adjoint_kernel(step, kind, info, *refs):
    if kind == "first":
        current, later, near, far, rate, injected, earlier, near_edge, far_edge, ext = refs
    elif kind == "third":
        (current, later, near, far, rate, injected, lap1, lap2, lap3,
         earlier, near_edge, far_edge, partial, ext) = refs
    else:
        current, later, near, far, rate, injected, earlier, ext = refs
    planes, nz, ny = current.shape
    place(ext, info, near, far)
    ext[pl.ds(halo, planes)] = rate[...] * current[...]
    group = group_of(planes, nz)
    along_y = band(ny, ny)
    along_z = band(group * nz, nz)
    for part in range(planes // group):
        first = part * group
        here = pl.ds(first, group)
        value = laplacian(ext, first, group, along_y, along_z)
        value = 2.0 * current[here] - later[here] + value + injected[step, here]
        earlier[here] = value
        if kind == "third":
            partial[here] = (
                later[here] * lap3[here] + current[here] * lap2[here] + value * lap1[here]
            )
    if kind != "last":
        near_at, far_at = edge_spots(info, planes)
        near_edge[...] = rate[pl.ds(near_at, halo)] * earlier[pl.ds(near_at, halo)]
        far_edge[...] = rate[pl.ds(far_at, halo)] * earlier[pl.ds(far_at, halo)]


def assemble_kernel(info, kept, got, total):
    half = kept.shape[0]
    mine = info[2] * half
    total[pl.ds(mine, half)] = kept[...]
    total[pl.ds(half - mine, half)] = got[...]


def swap(near_edge, far_edge):
    count = lax.axis_size("dom")
    near_pairs = [(i, i ^ 1) for i in range(count) if i ^ 1 < count]
    far_pairs = [(i, i + 1) for i in range(1, count - 1, 2)]
    far_pairs = far_pairs + [(b, a) for a, b in far_pairs]
    return (
        lax.ppermute(near_edge, "dom", near_pairs),
        lax.ppermute(far_edge, "dom", far_pairs),
    )


def per_device(
    wave_before,
    wave_current,
    adjoint_far,
    adjoint_near,
    labels,
    table,
    source_index,
    wavelet,
    receiver_index,
    residual,
):
    planes, nz, ny = wave_current.shape[1:]
    steps = wavelet.shape[1]
    place_x = lax.axis_index("dom")
    shot = lax.axis_index("shot")
    odd = place_x % 2
    info = jnp.stack([odd, place_x * planes, shot % 2]).astype(jnp.int32)
    u0, u1 = wave_before[0], wave_current[0]
    a6, a5 = adjoint_far[0], adjoint_near[0]
    block = f32(planes, nz, ny)
    edge = f32(halo, nz, ny)
    scratch = [pltpu.VMEM((planes + 2 * halo, nz, ny), jnp.float32)]
    cells = planes * nz * ny

    near_at = jnp.where(odd == 1, 0, planes - halo)
    near_edge = lax.dynamic_slice_in_dim(u1, near_at, halo, axis=0)
    far_edge = lax.dynamic_slice_in_dim(u1, planes - halo - near_at, halo, axis=0)
    u_halo = swap(near_edge, far_edge)

    rate, near_edge, far_edge = call(
        prepare_kernel, (info, table, labels, a5), [smem, smem, vmem, vmem], [block, edge, edge]
    )
    a_halo = swap(near_edge, far_edge)

    (injected,) = call(
        receivers_kernel,
        (info, receiver_index[0].T, residual[0]),
        [smem, vmem, vmem],
        [f32(steps, planes, nz, ny)],
        flops=2 * steps * 3 * cells * residual.shape[2],
    )

    work = 12 * cells * 256
    laps = []
    previous, current = u0, u1
    later, adjoint = a6, a5
    for n in range(steps):
        if n < steps - 1:
            upcoming, lap, near_edge, far_edge = call(
                functools.partial(forward_kernel, n, True),
                (info, source_index, wavelet, current, previous, *u_halo, rate),
                [smem] * 3 + [vmem] * 5,
                [block, block, edge, edge],
                scratch,
                work,
            )
            laps.append(lap)
            u_halo = swap(near_edge, far_edge)
        else:
            half = f32(planes // 2, nz, ny)
            upcoming, keep, send = call(
                functools.partial(forward_kernel, n, False),
                (info, source_index, wavelet, current, previous, *u_halo, rate, partial, a5),
                [smem] * 3 + [vmem] * 7,
                [block, half, half],
                scratch,
                work,
            )
        previous, current = current, upcoming
        step = steps - 1 - n
        if n == steps - 1:
            (earlier,) = call(
                functools.partial(adjoint_kernel, step, "last"),
                (info, adjoint, later, *a_halo, rate, injected),
                [smem] + [vmem] * 6,
                [block],
                scratch,
                work,
            )
        elif n == steps - 2:
            earlier, near_edge, far_edge, partial = call(
                functools.partial(adjoint_kernel, step, "third"),
                (info, adjoint, later, *a_halo, rate, injected, *laps),
                [smem] + [vmem] * 9,
                [block, edge, edge, block],
                scratch,
                work,
            )
            a_halo = swap(near_edge, far_edge)
        else:
            earlier, near_edge, far_edge = call(
                functools.partial(adjoint_kernel, step, "first"),
                (info, adjoint, later, *a_halo, rate, injected),
                [smem] + [vmem] * 6,
                [block, edge, edge],
                scratch,
                work,
            )
            a_halo = swap(near_edge, far_edge)
        later, adjoint = adjoint, earlier

    shots = lax.axis_size("shot")
    pairs = [(i, i ^ 1) for i in range(shots)]
    across = [(i, i ^ 2) for i in range(shots)]
    kept = keep + lax.ppermute(send, "shot", pairs)
    kept = kept + lax.ppermute(kept, "shot", across)
    got = lax.ppermute(kept, "shot", pairs)
    (total,) = call(
        assemble_kernel, (info, kept, got), [smem, vmem, vmem], [block]
    )
    return (current[None], adjoint[None], total)


def solution(mesh):
    placed = (
        P("shot", "dom", None, None),
        P("shot", "dom", None, None),
        P("shot", "dom", None, None),
        P("shot", "dom", None, None),
        P("dom", None, None),
        P(),
        P("shot", None),
        P("shot", None),
        P("shot", None, None),
        P("shot", None, None),
    )
    return jax.shard_map(
        per_device,
        mesh=mesh,
        in_specs=placed,
        out_specs=(
            P("shot", "dom", None, None),
            P("shot", "dom", None, None),
            P("dom", None, None),
        ),
        check_vma=False,
    )
```

```python
import functools

import jax
import jax.numpy as jnp
from jax import lax
from jax.experimental import pallas as pl
from jax.experimental.pallas import tpu as pltpu
from jax.sharding import PartitionSpec as P

centre_coef = -205.0 / 72.0
side_coefs = (8.0 / 5.0, -1.0 / 5.0, 8.0 / 315.0, -1.0 / 560.0)
unit = 5040.0
side_units = (8064.0, -1008.0, 128.0, -9.0)
halo = 4

vmem = pl.BlockSpec(memory_space=pltpu.VMEM)
smem = pl.BlockSpec(memory_space=pltpu.SMEM)
hbm = pl.BlockSpec(memory_space=pltpu.HBM)


def call(kernel, args, in_specs, outs, scratch=(), aliases={}):
    return pl.pallas_call(
        kernel,
        out_shape=[shape for shape, _ in outs],
        in_specs=in_specs,
        out_specs=[spec for _, spec in outs],
        scratch_shapes=list(scratch),
        input_output_aliases=aliases,
        compiler_params=pltpu.CompilerParams(vmem_limit_bytes=24 * 1024 * 1024),
        cost_estimate=pl.CostEstimate(flops=1024, bytes_accessed=1024, transcendentals=0),
    )(*args)


def f32(*shape):
    return jax.ShapeDtypeStruct(shape, jnp.float32)


def band(size, block):
    row = lax.broadcasted_iota(jnp.int32, (size, size), 0)
    col = lax.broadcasted_iota(jnp.int32, (size, size), 1)
    apart = jnp.abs(row - col)
    value = jnp.zeros((size, size), jnp.float32)
    for k in range(1, 5):
        value = jnp.where(apart == k, side_units[k - 1], value)
    if block != size:
        value = jnp.where(lax.div(row, block) == lax.div(col, block), value, 0.0)
    return value.astype(jnp.bfloat16)


def pieces(value):
    high = value.astype(jnp.bfloat16)
    rest = value - high.astype(jnp.float32)
    middle = rest.astype(jnp.bfloat16)
    low = (rest - middle.astype(jnp.float32)).astype(jnp.bfloat16)
    return high, middle, low


def dot(a, b):
    return lax.dot_general(a, b, (((1,), (0,)), ((), ())), preferred_element_type=jnp.float32)


def laplacian(field, at, along_y, along_z):
    _, nz, ny = field.shape
    centre = field[pl.ds(at, halo)]
    high, middle, low = pieces(centre.reshape(halo * nz, ny))
    across = dot(low, along_y) + dot(along_z, low)
    across = across + (dot(middle, along_y) + dot(along_z, middle))
    across = across + (dot(high, along_y) + dot(along_z, high))
    result = 3.0 * centre_coef * centre + across.reshape(halo, nz, ny) * (1.0 / unit)
    for k in range(1, 5):
        result = result + side_coefs[k - 1] * (
            field[pl.ds(at + k, halo)] + field[pl.ds(at - k, halo)]
        )
    return result


def bands(field):
    _, nz, ny = field.shape
    return band(ny, ny), band(halo * nz, nz)


def place(ext, info, near, far):
    planes = ext.shape[0] - 2 * halo
    odd = info[0]
    spot = jnp.where(odd == 1, 0, planes + halo)
    ext[pl.ds(spot, halo)] = near[...]
    ext[pl.ds(planes + halo - spot, halo)] = far[...]


def edge_spots(info, planes):
    odd = info[0]
    near = jnp.where(odd == 1, 0, planes - halo)
    return near, planes - halo - near


def add_source(field, first, info, source, value):
    count, _, ny = field.shape
    x = source[0, 0] - info[1] - first
    z = source[0, 1]
    y = source[0, 2]

    @pl.when((x >= 0) & (x < count))
    def _():
        base = pl.multiple_of(lax.div(z, 8) * 8, 8)
        rows = lax.broadcasted_iota(jnp.int32, (8, ny), 0)
        cols = lax.broadcasted_iota(jnp.int32, (8, ny), 1)
        hit = (rows == z - base) & (cols == y)
        tile = field[x, pl.ds(base, 8), :]
        field[x, pl.ds(base, 8), :] = tile + jnp.where(hit, value, 0.0)


def prepare_kernel(
    info, table, labels, near_field, *refs
):
    sources, refs = refs[:3], refs[3:]
    rate, near_edge, far_edge, field, *targets = refs[:7]
    label, sems = refs[7:]
    planes = labels.shape[0]
    first = pltpu.make_async_copy(labels, label, sems.at[0])
    second = pltpu.make_async_copy(near_field, field, sems.at[1])
    first.start()
    second.start()
    others = []
    for n in range(3):
        others.append(pltpu.make_async_copy(sources[n], targets[n], sems.at[2 + n]))
        others[n].start()
    first.wait()
    for part in range(planes // halo):
        here = pl.ds(part * halo, halo)
        known = label[here]
        value = jnp.zeros(known.shape, jnp.float32)
        for region in range(table.shape[0]):
            value = jnp.where(known == region, table[region], value)
        rate[here] = value
    second.wait()
    near, far = edge_spots(info, planes)
    near_edge[...] = rate[pl.ds(near, halo)] * field[pl.ds(near, halo)]
    far_edge[...] = rate[pl.ds(far, halo)] * field[pl.ds(far, halo)]
    for copy in others:
        copy.wait()


def receivers_kernel(info, index, values, injected):
    steps, planes, nz, ny = injected.shape
    count = index.shape[1]
    local = index[0:1, :] - info[1]
    cell = jnp.where((local >= 0) & (local < planes), local * nz + index[1:2, :], -1)
    at_y = lax.broadcasted_iota(jnp.int32, (ny, count), 0) == index[2:3, :]
    parts = []
    for step in range(steps):
        for piece in pieces(values[step : step + 1, :]):
            spread = jnp.where(at_y, piece.astype(jnp.float32), 0.0)
            parts.append(spread.astype(jnp.bfloat16))
    group = halo
    rows = group * nz
    for part in range(planes // group):
        at_cell = lax.broadcasted_iota(jnp.int32, (rows, count), 0) + part * rows == cell
        picked = jnp.where(at_cell, 1.0, 0.0).astype(jnp.bfloat16)
        for step in range(steps):
            total = None
            for piece in reversed(parts[3 * step : 3 * step + 3]):
                term = lax.dot_general(
                    picked, piece, (((1,), (1,)), ((), ())), preferred_element_type=jnp.float32
                )
                total = term if total is None else total + term
            injected[step, pl.ds(part * group, group)] = total.reshape(group, nz, ny)


def forward_kernel(step, info, source, wavelet, *refs):
    current, previous, near, far, rate, upcoming, lap, near_edge, far_edge, ext = refs
    planes = current.shape[0]
    place(ext, info, near, far)
    ext[pl.ds(halo, planes)] = current[...]
    along_y, along_z = bands(current)
    for first in range(0, planes, halo):
        here = pl.ds(first, halo)
        value = laplacian(ext, first + halo, along_y, along_z)
        lap[here] = value
        upcoming[here] = 2.0 * current[here] - previous[here] + rate[here] * value
    add_source(upcoming, 0, info, source, wavelet[0, step])
    near_at, far_at = edge_spots(info, planes)
    near_edge[...] = upcoming[pl.ds(near_at, halo)]
    far_edge[...] = upcoming[pl.ds(far_at, halo)]


def adjoint_kernel(step, info, *refs):
    current, later, near, far, rate, injected, earlier, near_edge, far_edge, ext = refs
    planes = current.shape[0]
    place(ext, info, near, far)
    ext[pl.ds(halo, planes)] = rate[...] * current[...]
    along_y, along_z = bands(current)
    for first in range(0, planes, halo):
        here = pl.ds(first, halo)
        value = laplacian(ext, first + halo, along_y, along_z)
        earlier[here] = 2.0 * current[here] - later[here] + value + injected[step, here]
    near_at, far_at = edge_spots(info, planes)
    near_edge[...] = rate[pl.ds(near_at, halo)] * earlier[pl.ds(near_at, halo)]
    far_edge[...] = rate[pl.ds(far_at, halo)] * earlier[pl.ds(far_at, halo)]


def turn_kernel(forward_step, step, info, source, wavelet, *refs):
    (current, later, near, far, rate, injected, lap1, lap2, lap3, wave, before, a5,
     earlier, near_edge, far_edge, rest, keep, send, final, ext, stage, grad, sem) = refs
    planes = current.shape[0]
    place(ext, info, near, far)
    ext[pl.ds(halo, planes)] = rate[...] * current[...]
    along_y, along_z = bands(current)
    for first in range(0, planes, halo):
        here = pl.ds(first, halo)
        value = laplacian(ext, first + halo, along_y, along_z)
        value = 2.0 * current[here] - later[here] + value + injected[step, here]
        earlier[here] = value
        partial = later[here] * lap3[here] + current[here] * lap2[here] + value * lap1[here]
        if first == 0:
            rest[0] = partial
        elif first == planes - halo:
            rest[1] = partial
        else:
            value = laplacian(wave, first, along_y, along_z)
            inner = pl.ds(first - halo, halo)
            stage[inner] = 2.0 * wave[here] - before[here] + rate[here] * value
            grad[inner] = partial + a5[here] * value
    add_source(stage, halo, info, source, wavelet[0, forward_step])
    copy = pltpu.make_async_copy(stage, final.at[pl.ds(halo, planes - 2 * halo)], sem)
    copy.start()
    near_at, far_at = edge_spots(info, planes)
    near_edge[...] = rate[pl.ds(near_at, halo)] * earlier[pl.ds(near_at, halo)]
    far_edge[...] = rate[pl.ds(far_at, halo)] * earlier[pl.ds(far_at, halo)]
    half = keep.shape[0]
    mine = info[2] * half
    keep[...] = grad[pl.ds(mine, half)]
    send[...] = grad[pl.ds(half - mine, half)]
    copy.wait()


def forward_outer_kernel(step, info, source, wavelet, *refs):
    (current, previous, near, far, rate, rest, a5, _,
     keep, send, final, ext, stage, grad, sems) = refs
    planes = current.shape[0]
    place(ext, info, near, far)
    ext[pl.ds(halo, planes)] = current[...]
    along_y, along_z = bands(current)
    copies = []
    for side, first in enumerate((0, planes - halo)):
        here = pl.ds(first, halo)
        value = laplacian(ext, first + halo, along_y, along_z)
        stage[side] = 2.0 * current[here] - previous[here] + rate[here] * value
        grad[side] = rest[side] + a5[here] * value
        add_source(stage.at[side], first, info, source, wavelet[0, step])
        copies.append(pltpu.make_async_copy(stage.at[side], final.at[here], sems.at[side]))
        copies[side].start()
    keep[...] = grad[info[2]]
    send[...] = grad[1 - info[2]]
    for copy in copies:
        copy.wait()


def adjoint_inner_kernel(step, info, current, later, rate, injected, first_adjoint, ext, stage, sem):
    planes = current.shape[0]
    ext[...] = rate[...] * current[...]
    along_y, along_z = bands(current)
    for first in range(halo, planes - halo, halo):
        here = pl.ds(first, halo)
        value = laplacian(ext, first, along_y, along_z)
        stage[pl.ds(first - halo, halo)] = (
            2.0 * current[here] - later[here] + value + injected[step, here]
        )
    copy = pltpu.make_async_copy(stage, first_adjoint.at[pl.ds(halo, planes - 2 * halo)], sem)
    copy.start()
    copy.wait()


def adjoint_outer_kernel(step, info, *refs):
    current, later, near, far, rate, injected, _, first_adjoint, ext, stage, sems = refs
    planes = current.shape[0]
    place(ext, info, near, far)
    ext[pl.ds(halo, planes)] = rate[...] * current[...]
    along_y, along_z = bands(current)
    copies = []
    for side, first in enumerate((0, planes - halo)):
        here = pl.ds(first, halo)
        value = laplacian(ext, first + halo, along_y, along_z)
        stage[side] = 2.0 * current[here] - later[here] + value + injected[step, here]
        copies.append(pltpu.make_async_copy(stage.at[side], first_adjoint.at[here], sems.at[side]))
        copies[side].start()
    for copy in copies:
        copy.wait()


def assemble_kernel(info, inner_kept, inner_got, kept, got, total, sems):
    planes = total.shape[0]
    half = inner_kept.shape[0]
    mine = info[2] * half
    side = info[2] * (planes - halo)
    spots = (
        (inner_kept, halo + mine, half),
        (inner_got, halo + half - mine, half),
        (kept, side, halo),
        (got, planes - halo - side, halo),
    )
    copies = []
    for n, (piece, at, count) in enumerate(spots):
        copies.append(pltpu.make_async_copy(piece, total.at[pl.ds(at, count)], sems.at[n]))
        copies[n].start()
    for copy in copies:
        copy.wait()


def swap(near_edge, far_edge):
    count = lax.axis_size("dom")
    near_pairs = [(i, i ^ 1) for i in range(count) if i ^ 1 < count]
    far_pairs = [(i, i + 1) for i in range(1, count - 1, 2)]
    far_pairs = far_pairs + [(b, a) for a, b in far_pairs]
    return (
        lax.ppermute(near_edge, "dom", near_pairs),
        lax.ppermute(far_edge, "dom", far_pairs),
    )


def summed(keep, send):
    shots = lax.axis_size("shot")
    pairs = [(i, i ^ 1) for i in range(shots)]
    across = [(i, i ^ 2) for i in range(shots)]
    kept = keep + lax.ppermute(send, "shot", pairs)
    kept = kept + lax.ppermute(kept, "shot", across)
    return kept, lax.ppermute(kept, "shot", pairs)


def per_device(
    wave_before,
    wave_current,
    adjoint_far,
    adjoint_near,
    labels,
    table,
    source_index,
    wavelet,
    receiver_index,
    residual,
):
    planes, nz, ny = wave_current.shape[1:]
    steps = wavelet.shape[1]
    place_x = lax.axis_index("dom")
    odd = place_x % 2
    info = jnp.stack([odd, place_x * planes, lax.axis_index("shot") % 2]).astype(jnp.int32)
    u0, u1 = wave_before[0], wave_current[0]
    a6, a5 = adjoint_far[0], adjoint_near[0]
    whole = f32(planes, nz, ny)
    block = (whole, vmem)
    edge = (f32(halo, nz, ny), vmem)
    inner = planes - 2 * halo
    quarter = (f32(inner // 2, nz, ny), vmem)
    ext = pltpu.VMEM((planes + 2 * halo, nz, ny), jnp.float32)
    within = pltpu.VMEM((inner, nz, ny), jnp.float32)
    outer = pltpu.VMEM((2, halo, nz, ny), jnp.float32)

    near_at = jnp.where(odd == 1, 0, planes - halo)
    near_edge = lax.dynamic_slice_in_dim(u1, near_at, halo, axis=0)
    far_edge = lax.dynamic_slice_in_dim(u1, planes - halo - near_at, halo, axis=0)
    u_halo = swap(near_edge, far_edge)

    rate, near_edge, far_edge, a5, u1, u0, a6 = call(
        prepare_kernel,
        (info, table, labels, a5, u1, u0, a6),
        [smem, smem] + [hbm] * 5,
        [block, edge, edge] + [block] * 4,
        [pltpu.VMEM((planes, nz, ny), jnp.int32), pltpu.SemaphoreType.DMA((5,))],
    )
    a_halo = swap(near_edge, far_edge)

    (injected,) = call(
        receivers_kernel,
        (info, receiver_index[0].T, residual[0]),
        [smem, vmem, vmem],
        [(f32(steps, planes, nz, ny), vmem)],
    )

    laps = []
    previous, current = u0, u1
    later, adjoint = a6, a5
    for n in range(steps - 1):
        upcoming, lap, near_edge, far_edge = call(
            functools.partial(forward_kernel, n),
            (info, source_index, wavelet, current, previous, *u_halo, rate),
            [smem] * 3 + [vmem] * 5,
            [block, block, edge, edge],
            [ext],
        )
        laps.append(lap)
        u_halo = swap(near_edge, far_edge)
        previous, current = current, upcoming
        step = steps - 1 - n
        if n < steps - 2:
            earlier, near_edge, far_edge = call(
                functools.partial(adjoint_kernel, step),
                (info, adjoint, later, *a_halo, rate, injected),
                [smem] + [vmem] * 6,
                [block, edge, edge],
                [ext],
            )
        else:
            earlier, near_edge, far_edge, rest, keep, send, final = call(
                functools.partial(turn_kernel, steps - 1, step),
                (info, source_index, wavelet, adjoint, later, *a_halo, rate, injected, *laps,
                 current, previous, a5),
                [smem] * 3 + [vmem] * 12,
                [block, edge, edge, (f32(2, halo, nz, ny), vmem), quarter, quarter, (whole, hbm)],
                [ext, within, within, pltpu.SemaphoreType.DMA],
            )
        a_halo = swap(near_edge, far_edge)
        later, adjoint = adjoint, earlier

    inner_kept, inner_got = summed(keep, send)
    keep, send, final = call(
        functools.partial(forward_outer_kernel, steps - 1),
        (info, source_index, wavelet, current, previous, *u_halo, rate, rest, a5, final),
        [smem] * 3 + [vmem] * 7 + [hbm],
        [edge, edge, (whole, hbm)],
        [ext, outer, outer, pltpu.SemaphoreType.DMA((2,))],
        {10: 2},
    )
    kept, got = summed(keep, send)
    (first_adjoint,) = call(
        functools.partial(adjoint_inner_kernel, 0),
        (info, adjoint, later, rate, injected),
        [smem] + [vmem] * 4,
        [(whole, hbm)],
        [pltpu.VMEM((planes, nz, ny), jnp.float32), within, pltpu.SemaphoreType.DMA],
    )
    (first_adjoint,) = call(
        functools.partial(adjoint_outer_kernel, 0),
        (info, adjoint, later, *a_halo, rate, injected, first_adjoint),
        [smem] + [vmem] * 6 + [hbm],
        [(whole, hbm)],
        [ext, outer, pltpu.SemaphoreType.DMA((2,))],
        {7: 0},
    )
    (total,) = call(
        assemble_kernel,
        (info, inner_kept, inner_got, kept, got),
        [smem] + [vmem] * 4,
        [(whole, hbm)],
        [pltpu.SemaphoreType.DMA((4,))],
    )
    return (final[None], first_adjoint[None], total)


def solution(mesh):
    placed = (
        P("shot", "dom", None, None),
        P("shot", "dom", None, None),
        P("shot", "dom", None, None),
        P("shot", "dom", None, None),
        P("dom", None, None),
        P(),
        P("shot", None),
        P("shot", None),
        P("shot", None, None),
        P("shot", None, None),
    )
    return jax.shard_map(
        per_device,
        mesh=mesh,
        in_specs=placed,
        out_specs=(
            P("shot", "dom", None, None),
            P("shot", "dom", None, None),
            P("dom", None, None),
        ),
        check_vma=False,
    )
```

```python
import functools

import jax
import jax.numpy as jnp
from jax import lax
from jax.experimental import pallas as pl
from jax.experimental.pallas import tpu as pltpu
from jax.sharding import PartitionSpec as P

centre_coef = -205.0 / 72.0
side_coefs = (8.0 / 5.0, -1.0 / 5.0, 8.0 / 315.0, -1.0 / 560.0)
unit = 5040.0
side_units = (8064.0, -1008.0, 128.0, -9.0)
halo = 4

vmem = pl.BlockSpec(memory_space=pltpu.VMEM)
hbm = pl.BlockSpec(memory_space=pltpu.HBM)
wherever = pl.BlockSpec(memory_space=pl.ANY)


def call(kernel, args, in_specs, outs, scratch=(), aliases={}, limit=24, cost=1024):
    return pl.pallas_call(
        kernel,
        out_shape=[
            pltpu.VMEM(shape.shape, shape.dtype) if spec is vmem else shape for shape, spec in outs
        ],
        in_specs=in_specs,
        out_specs=[spec for _, spec in outs],
        scratch_shapes=list(scratch),
        input_output_aliases=aliases,
        compiler_params=pltpu.CompilerParams(vmem_limit_bytes=limit * 1024 * 1024),
        cost_estimate=pl.CostEstimate(flops=cost, bytes_accessed=1024, transcendentals=0),
    )(*args)


def f32(*shape):
    return jax.ShapeDtypeStruct(shape, jnp.float32)


def band(size, block):
    row = lax.broadcasted_iota(jnp.int32, (size, size), 0)
    col = lax.broadcasted_iota(jnp.int32, (size, size), 1)
    apart = jnp.abs(row - col)
    value = jnp.zeros((size, size), jnp.float32)
    for k in range(1, 5):
        value = jnp.where(apart == k, side_units[k - 1], value)
    if block != size:
        value = jnp.where(lax.div(row, block) == lax.div(col, block), value, 0.0)
    return value.astype(jnp.bfloat16)


def pieces(value):
    high = value.astype(jnp.bfloat16)
    rest = value - high.astype(jnp.float32)
    middle = rest.astype(jnp.bfloat16)
    low = (rest - middle.astype(jnp.float32)).astype(jnp.bfloat16)
    return high, middle, low


def dot(a, b):
    return lax.dot_general(a, b, (((1,), (0,)), ((), ())), preferred_element_type=jnp.float32)


def laplacian(field, at, along_y, along_z):
    _, nz, ny = field.shape
    centre = field[pl.ds(at, halo)]
    high, middle, low = pieces(centre.reshape(halo * nz, ny))
    across = dot(low, along_y) + dot(along_z, low)
    across = across + (dot(middle, along_y) + dot(along_z, middle))
    across = across + (dot(high, along_y) + dot(along_z, high))
    result = 3.0 * centre_coef * centre + across.reshape(halo, nz, ny) * (1.0 / unit)
    for k in range(1, 5):
        result = result + side_coefs[k - 1] * (
            field[pl.ds(at + k, halo)] + field[pl.ds(at - k, halo)]
        )
    return result


def bands(field):
    _, nz, ny = field.shape
    return band(ny, ny), band(halo * nz, nz)


def core():
    return lax.axis_index("shot") % 2


def place(ext, near, far):
    planes = ext.shape[0] - 2 * halo
    odd = lax.axis_index("dom") % 2
    spot = jnp.where(odd == 1, 0, planes + halo)
    ext[pl.ds(spot, halo)] = near[...]
    ext[pl.ds(planes + halo - spot, halo)] = far[...]


def edge_spots(planes):
    odd = lax.axis_index("dom") % 2
    near = jnp.where(odd == 1, 0, planes - halo)
    return near, planes - halo - near


def add_source(field, first, planes, source, value):
    count, _, ny = field.shape
    x = source[0, 0] - lax.axis_index("dom") * planes - first
    z = source[0, 1]
    y = source[0, 2]

    @pl.when((x >= 0) & (x < count))
    def _():
        base = pl.multiple_of(lax.div(z, 8) * 8, 8)
        rows = lax.broadcasted_iota(jnp.int32, (8, ny), 0)
        cols = lax.broadcasted_iota(jnp.int32, (8, ny), 1)
        hit = (rows == z - base) & (cols == y)
        tile = field[x, pl.ds(base, 8), :]
        field[x, pl.ds(base, 8), :] = tile + jnp.where(hit, value, 0.0)


def prepare_kernel(
    table, labels, near_field, *refs
):
    sources, refs = refs[:3], refs[3:]
    rate, near_edge, far_edge, field, *targets = refs[:7]
    label, sems = refs[7:]
    planes = labels.shape[0]
    first = pltpu.make_async_copy(labels, label, sems.at[0])
    second = pltpu.make_async_copy(near_field, field, sems.at[1])
    first.start()
    second.start()
    others = []
    for n in range(3):
        others.append(pltpu.make_async_copy(sources[n], targets[n], sems.at[2 + n]))
        others[n].start()
    first.wait()
    for part in range(planes // halo):
        here = pl.ds(part * halo, halo)
        known = label[here]
        value = jnp.zeros(known.shape, jnp.float32)
        for region in range(table.shape[0]):
            value = jnp.where(known == region, table[region], value)
        rate[here] = value
    second.wait()
    near, far = edge_spots(planes)
    near_edge[...] = rate[pl.ds(near, halo)] * field[pl.ds(near, halo)]
    far_edge[...] = rate[pl.ds(far, halo)] * field[pl.ds(far, halo)]
    for copy in others:
        copy.wait()


def receivers_kernel(index, values, _, injected):
    steps, planes, nz, ny = injected.shape
    count = index.shape[1]
    local = index[0:1, :] - lax.axis_index("dom") * planes
    cell = jnp.where((local >= 0) & (local < planes), local * nz + index[1:2, :], -1)
    at_y = lax.broadcasted_iota(jnp.int32, (ny, count), 0) == index[2:3, :]
    parts = []
    for step in range(steps):
        for piece in pieces(values[step : step + 1, :]):
            spread = jnp.where(at_y, piece.astype(jnp.float32), 0.0)
            parts.append(spread.astype(jnp.bfloat16))
    group = halo
    rows = group * nz
    for part in range(planes // group):
        at_cell = lax.broadcasted_iota(jnp.int32, (rows, count), 0) + part * rows == cell
        picked = jnp.where(at_cell, 1.0, 0.0).astype(jnp.bfloat16)
        for step in range(steps):
            total = None
            for piece in reversed(parts[3 * step : 3 * step + 3]):
                term = lax.dot_general(
                    picked, piece, (((1,), (1,)), ((), ())), preferred_element_type=jnp.float32
                )
                total = term if total is None else total + term
            injected[step, pl.ds(part * group, group)] = total.reshape(group, nz, ny)


def forward_kernel(step, source, wavelet, *refs):
    current, previous, near, far, rate, _, upcoming, lap, near_edge, far_edge, ext = refs
    planes = current.shape[0]
    place(ext, near, far)
    ext[pl.ds(halo, planes)] = current[...]
    along_y, along_z = bands(current)
    for first in range(0, planes, halo):
        here = pl.ds(first, halo)
        value = laplacian(ext, first + halo, along_y, along_z)
        lap[here] = value
        upcoming[here] = 2.0 * current[here] - previous[here] + rate[here] * value
    add_source(upcoming, 0, planes, source, wavelet[0, step])
    near_at, far_at = edge_spots(planes)
    near_edge[...] = upcoming[pl.ds(near_at, halo)]
    far_edge[...] = upcoming[pl.ds(far_at, halo)]


def adjoint_kernel(step, *refs):
    current, later, near, far, rate, injected, earlier, near_edge, far_edge, ext = refs
    planes = current.shape[0]
    place(ext, near, far)
    ext[pl.ds(halo, planes)] = rate[...] * current[...]
    along_y, along_z = bands(current)
    for first in range(0, planes, halo):
        here = pl.ds(first, halo)
        value = laplacian(ext, first + halo, along_y, along_z)
        earlier[here] = 2.0 * current[here] - later[here] + value + injected[step, here]
    near_at, far_at = edge_spots(planes)
    near_edge[...] = rate[pl.ds(near_at, halo)] * earlier[pl.ds(near_at, halo)]
    far_edge[...] = rate[pl.ds(far_at, halo)] * earlier[pl.ds(far_at, halo)]


def turn_kernel(forward_step, step, source, wavelet, *refs):
    (current, later, near, far, rate, injected, lap1, lap2, lap3, wave, before, a5,
     earlier, near_edge, far_edge, rest, keep, send, inner, ext, grad) = refs
    planes = current.shape[0]
    place(ext, near, far)
    ext[pl.ds(halo, planes)] = rate[...] * current[...]
    along_y, along_z = bands(current)
    for first in range(0, planes, halo):
        here = pl.ds(first, halo)
        value = laplacian(ext, first + halo, along_y, along_z)
        value = 2.0 * current[here] - later[here] + value + injected[step, here]
        earlier[here] = value
        partial = later[here] * lap3[here] + current[here] * lap2[here] + value * lap1[here]
        if first == 0:
            rest[0] = partial
        elif first == planes - halo:
            rest[1] = partial
        else:
            value = laplacian(wave, first, along_y, along_z)
            within = pl.ds(first - halo, halo)
            inner[within] = 2.0 * wave[here] - before[here] + rate[here] * value
            grad[within] = partial + a5[here] * value
    add_source(inner, halo, planes, source, wavelet[0, forward_step])
    near_at, far_at = edge_spots(planes)
    near_edge[...] = rate[pl.ds(near_at, halo)] * earlier[pl.ds(near_at, halo)]
    far_edge[...] = rate[pl.ds(far_at, halo)] * earlier[pl.ds(far_at, halo)]
    half = keep.shape[0]
    mine = core() * half
    keep[...] = grad[pl.ds(mine, half)]
    send[...] = grad[pl.ds(half - mine, half)]


def forward_outer_kernel(step, source, wavelet, *refs):
    current, previous, near, far, rate, rest, a5, keep, send, outer, ext, grad = refs
    planes = current.shape[0]
    place(ext, near, far)
    ext[pl.ds(halo, planes)] = current[...]
    along_y, along_z = bands(current)
    for side, first in enumerate((0, planes - halo)):
        here = pl.ds(first, halo)
        value = laplacian(ext, first + halo, along_y, along_z)
        outer[side] = 2.0 * current[here] - previous[here] + rate[here] * value
        grad[side] = rest[side] + a5[here] * value
        add_source(outer.at[side], first, planes, source, wavelet[0, step])
    keep[...] = grad[core()]
    send[...] = grad[1 - core()]


def adjoint_inner_kernel(step, *refs):
    (current, later, rate, injected, inner, near_in, far_in, _,
     first_adjoint, final, near_edge, far_edge, ext, stage, sems) = refs
    planes = current.shape[0]
    within = pl.ds(halo, planes - 2 * halo)
    wave_copy = pltpu.make_async_copy(inner, final.at[within], sems.at[0])
    wave_copy.start()
    ext[...] = rate[...] * current[...]
    along_y, along_z = bands(current)
    for first in range(halo, planes - halo, halo):
        here = pl.ds(first, halo)
        value = laplacian(ext, first, along_y, along_z)
        stage[pl.ds(first - halo, halo)] = (
            2.0 * current[here] - later[here] + value + injected[step, here]
        )
    copy = pltpu.make_async_copy(stage, first_adjoint.at[within], sems.at[1])
    copy.start()
    near_edge[...] = near_in[...]
    far_edge[...] = far_in[...]
    wave_copy.wait()
    copy.wait()


def adjoint_outer_kernel(step, *refs):
    (current, later, near, far, rate, injected, outer, _, _,
     first_adjoint, final, token, ext, stage, sems) = refs
    planes = current.shape[0]
    copies = []
    for side, first in enumerate((0, planes - halo)):
        here = pl.ds(first, halo)
        copies.append(pltpu.make_async_copy(outer.at[side], final.at[here], sems.at[side]))
        copies[-1].start()
    place(ext, near, far)
    ext[pl.ds(halo, planes)] = rate[...] * current[...]
    along_y, along_z = bands(current)
    for side, first in enumerate((0, planes - halo)):
        here = pl.ds(first, halo)
        value = laplacian(ext, first + halo, along_y, along_z)
        stage[side] = 2.0 * current[here] - later[here] + value + injected[step, here]
        copies.append(
            pltpu.make_async_copy(stage.at[side], first_adjoint.at[here], sems.at[2 + side])
        )
        copies[-1].start()
    token[...] = jnp.zeros_like(token)
    for copy in copies:
        copy.wait()


def assemble_kernel(inner_kept, inner_got, kept, got, total, sems):
    planes = total.shape[0]
    half = inner_kept.shape[0]
    mine = core() * half
    side = core() * (planes - halo)
    spots = (
        (inner_kept, halo + mine, half),
        (inner_got, halo + half - mine, half),
        (kept, side, halo),
        (got, planes - halo - side, halo),
    )
    copies = []
    for n, (piece, at, count) in enumerate(spots):
        copies.append(pltpu.make_async_copy(piece, total.at[pl.ds(at, count)], sems.at[n]))
        copies[n].start()
    for copy in copies:
        copy.wait()


def swap(near_edge, far_edge):
    count = lax.axis_size("dom")
    near_pairs = [(i, i ^ 1) for i in range(count) if i ^ 1 < count]
    far_pairs = [(i, i + 1) for i in range(1, count - 1, 2)]
    far_pairs = far_pairs + [(b, a) for a, b in far_pairs]
    return (
        lax.ppermute(near_edge, "dom", near_pairs),
        lax.ppermute(far_edge, "dom", far_pairs),
    )


def parts_kernel(keep, *refs):
    parts, total = refs[:-2], refs[-1]
    size = parts[0].shape[0]
    for n, part in enumerate(parts):
        here = pl.ds(n * size, size)
        total[here] = keep[here] + part[...]


def add_kernel(a, b, _, total):
    total[...] = a[...] + b[...]


def first_sum(keep, send, after, count):
    shots = lax.axis_size("shot")
    pairs = [(i, i ^ 1) for i in range(shots)]
    across = [(i, i ^ 2) for i in range(shots)]
    size = send.shape[0] // count
    got = [lax.ppermute(send[n * size : (n + 1) * size], "shot", pairs) for n in range(count)]
    (kept,) = call(
        parts_kernel,
        (keep, *got, after),
        [vmem] * (1 + count) + [wherever],
        [(jax.ShapeDtypeStruct(keep.shape, jnp.float32), vmem)],
    )
    return kept, lax.ppermute(kept, "shot", across)


def second_sum(kept, got, after):
    shots = lax.axis_size("shot")
    pairs = [(i, i ^ 1) for i in range(shots)]
    (kept,) = call(
        add_kernel,
        (kept, got, after),
        [vmem, vmem, wherever],
        [(jax.ShapeDtypeStruct(kept.shape, jnp.float32), vmem)],
    )
    return kept, lax.ppermute(kept, "shot", pairs)


def per_device(
    wave_before,
    wave_current,
    adjoint_far,
    adjoint_near,
    labels,
    table,
    source_index,
    wavelet,
    receiver_index,
    residual,
):
    planes, nz, ny = wave_current.shape[1:]
    steps = wavelet.shape[1]
    odd = lax.axis_index("dom") % 2
    u0, u1 = wave_before[0], wave_current[0]
    a6, a5 = adjoint_far[0], adjoint_near[0]
    u0, u1, a6, a5, labels = (
        pltpu.with_memory_space_constraint(x, pltpu.HBM) for x in (u0, u1, a6, a5, labels)
    )
    whole = f32(planes, nz, ny)
    block = (whole, vmem)
    edge = (f32(halo, nz, ny), vmem)
    inner = planes - 2 * halo
    quarter = (f32(inner // 2, nz, ny), vmem)
    pair = (f32(2, halo, nz, ny), vmem)
    ext = pltpu.VMEM((planes + 2 * halo, nz, ny), jnp.float32)
    within = pltpu.VMEM((inner, nz, ny), jnp.float32)
    outer = pltpu.VMEM((2, halo, nz, ny), jnp.float32)

    near_at = jnp.where(odd == 1, 0, planes - halo)
    near_edge = lax.dynamic_slice_in_dim(wave_current[0], near_at, halo, axis=0)
    far_edge = lax.dynamic_slice_in_dim(wave_current[0], planes - halo - near_at, halo, axis=0)
    u_halo = swap(near_edge, far_edge)

    rate, near_edge, far_edge, a5, u1, u0, a6 = call(
        prepare_kernel,
        (table, labels, a5, u1, u0, a6),
        [vmem] + [hbm] * 5,
        [block, edge, edge] + [block] * 4,
        [pltpu.VMEM((planes, nz, ny), jnp.int32), pltpu.SemaphoreType.DMA((5,))],
    )
    a_halo = swap(near_edge, far_edge)

    (injected,) = call(
        receivers_kernel,
        (receiver_index[0].T, residual[0], rate),
        [vmem, vmem, wherever],
        [(f32(steps, planes, nz, ny), vmem)],
    )

    laps = []
    previous, current = u0, u1
    later, adjoint = a6, a5
    for n in range(steps - 1):
        upcoming, lap, near_edge, far_edge = call(
            functools.partial(forward_kernel, n),
            (source_index, wavelet, current, previous, *u_halo, rate, injected),
            [vmem] * 7 + [wherever],
            [block, block, edge, edge],
            [ext],
        )
        laps.append(lap)
        u_halo = swap(near_edge, far_edge)
        previous, current = current, upcoming
        step = steps - 1 - n
        if n < steps - 2:
            earlier, near_edge, far_edge = call(
                functools.partial(adjoint_kernel, step),
                (adjoint, later, *a_halo, rate, injected),
                [vmem] * 6,
                [block, edge, edge],
                [ext],
            )
        else:
            earlier, near_edge, far_edge, rest, keep, send, inner_wave = call(
                functools.partial(turn_kernel, steps - 1, step),
                (source_index, wavelet, adjoint, later, *a_halo, rate, injected, *laps,
                 current, previous, a5),
                [vmem] * 14,
                [block, edge, edge, pair, quarter, quarter, (f32(inner, nz, ny), vmem)],
                [ext, within],
            )
        if n < steps - 2:
            a_halo = swap(near_edge, far_edge)
        later, adjoint = adjoint, earlier

    inner_sum = first_sum(keep, send, keep, 4)
    first_adjoint, final, near_edge, far_edge = call(
        functools.partial(adjoint_inner_kernel, 0),
        (adjoint, later, rate, injected, inner_wave, near_edge, far_edge, inner_sum[0]),
        [vmem] * 7 + [wherever],
        [(whole, hbm), (whole, hbm), edge, edge],
        [pltpu.VMEM((planes, nz, ny), jnp.float32), within, pltpu.SemaphoreType.DMA((2,))],
    )
    a_halo = swap(near_edge, far_edge)
    keep, send, outer_wave = call(
        functools.partial(forward_outer_kernel, steps - 1),
        (source_index, wavelet, current, previous, *u_halo, rate, rest, a5),
        [vmem] * 9,
        [edge, edge, pair],
        [ext, outer],
    )
    outer_sum = first_sum(keep, send, inner_sum[1], 2)
    first_adjoint, final, token = call(
        functools.partial(adjoint_outer_kernel, 0),
        (adjoint, later, *a_halo, rate, injected, outer_wave, first_adjoint, final),
        [vmem] * 7 + [hbm] * 2,
        [(whole, hbm), (whole, hbm), (f32(8, 128), vmem)],
        [ext, outer, pltpu.SemaphoreType.DMA((4,))],
        {7: 0, 8: 1},
        cost=2000000000,
    )
    inner_kept, inner_got = second_sum(*inner_sum, token)
    kept, got = second_sum(*outer_sum, token)
    (total,) = call(
        assemble_kernel,
        (inner_kept, inner_got, kept, got),
        [vmem] * 4,
        [(whole, hbm)],
        [pltpu.SemaphoreType.DMA((4,))],
    )
    return (final[None], first_adjoint[None], total)


def solution(mesh):
    placed = (
        P("shot", "dom", None, None),
        P("shot", "dom", None, None),
        P("shot", "dom", None, None),
        P("shot", "dom", None, None),
        P("dom", None, None),
        P(),
        P("shot", None),
        P("shot", None),
        P("shot", None, None),
        P("shot", None, None),
    )
    return jax.shard_map(
        per_device,
        mesh=mesh,
        in_specs=placed,
        out_specs=(
            P("shot", "dom", None, None),
            P("shot", "dom", None, None),
            P("dom", None, None),
        ),
        check_vma=False,
    )
```

```python
import functools

import jax
import jax.numpy as jnp
from jax import lax
from jax.experimental import pallas as pl
from jax.experimental.pallas import tpu as pltpu
from jax.sharding import PartitionSpec as P

centre_coef = -205.0 / 72.0
side_coefs = (8.0 / 5.0, -1.0 / 5.0, 8.0 / 315.0, -1.0 / 560.0)
unit = 5040.0
side_units = (8064.0, -1008.0, 128.0, -9.0)
halo = 4

vmem = pl.BlockSpec(memory_space=pltpu.VMEM)
hbm = pl.BlockSpec(memory_space=pltpu.HBM)
wherever = pl.BlockSpec(memory_space=pl.ANY)


def call(kernel, args, in_specs, outs, scratch=(), aliases={}, limit=24, cost=1024):
    return pl.pallas_call(
        kernel,
        out_shape=[
            pltpu.VMEM(shape.shape, shape.dtype) if spec is vmem else shape for shape, spec in outs
        ],
        in_specs=in_specs,
        out_specs=[spec for _, spec in outs],
        scratch_shapes=list(scratch),
        input_output_aliases=aliases,
        compiler_params=pltpu.CompilerParams(vmem_limit_bytes=limit * 1024 * 1024),
        cost_estimate=pl.CostEstimate(flops=cost, bytes_accessed=1024, transcendentals=0),
    )(*args)


def f32(*shape):
    return jax.ShapeDtypeStruct(shape, jnp.float32)


def band(size, block):
    row = lax.broadcasted_iota(jnp.int32, (size, size), 0)
    col = lax.broadcasted_iota(jnp.int32, (size, size), 1)
    apart = jnp.abs(row - col)
    value = jnp.zeros((size, size), jnp.float32)
    for k in range(1, 5):
        value = jnp.where(apart == k, side_units[k - 1], value)
    if block != size:
        value = jnp.where(lax.div(row, block) == lax.div(col, block), value, 0.0)
    return value.astype(jnp.bfloat16)


def pieces(value):
    high = value.astype(jnp.bfloat16)
    rest = value - high.astype(jnp.float32)
    middle = rest.astype(jnp.bfloat16)
    low = (rest - middle.astype(jnp.float32)).astype(jnp.bfloat16)
    return high, middle, low


def dot(a, b):
    return lax.dot_general(a, b, (((1,), (0,)), ((), ())), preferred_element_type=jnp.float32)


def laplacian(field, at, along_y, along_z):
    _, nz, ny = field.shape
    centre = field[pl.ds(at, halo)]
    high, middle, low = pieces(centre.reshape(halo * nz, ny))
    across = dot(low, along_y) + dot(along_z, low)
    across = across + (dot(middle, along_y) + dot(along_z, middle))
    across = across + (dot(high, along_y) + dot(along_z, high))
    result = 3.0 * centre_coef * centre + across.reshape(halo, nz, ny) * (1.0 / unit)
    for k in range(1, 5):
        result = result + side_coefs[k - 1] * (
            field[pl.ds(at + k, halo)] + field[pl.ds(at - k, halo)]
        )
    return result


def bands(field):
    _, nz, ny = field.shape
    return band(ny, ny), band(halo * nz, nz)


def core():
    return lax.axis_index("shot") % 2


def place(ext, near, far):
    planes = ext.shape[0] - 2 * halo
    odd = lax.axis_index("dom") % 2
    spot = jnp.where(odd == 1, 0, planes + halo)
    ext[pl.ds(spot, halo)] = near[...]
    ext[pl.ds(planes + halo - spot, halo)] = far[...]


def edge_spots(planes):
    odd = lax.axis_index("dom") % 2
    near = jnp.where(odd == 1, 0, planes - halo)
    return near, planes - halo - near


def add_source(field, first, planes, source, value):
    count, _, ny = field.shape
    x = source[0, 0] - lax.axis_index("dom") * planes - first
    z = source[0, 1]
    y = source[0, 2]

    @pl.when((x >= 0) & (x < count))
    def _():
        base = pl.multiple_of(lax.div(z, 8) * 8, 8)
        rows = lax.broadcasted_iota(jnp.int32, (8, ny), 0)
        cols = lax.broadcasted_iota(jnp.int32, (8, ny), 1)
        hit = (rows == z - base) & (cols == y)
        tile = field[x, pl.ds(base, 8), :]
        field[x, pl.ds(base, 8), :] = tile + jnp.where(hit, value, 0.0)


def prepare_kernel(
    table, labels, near_field, *refs
):
    sources, refs = refs[:3], refs[3:]
    rate, near_edge, far_edge, field, *targets = refs[:7]
    label, sems = refs[7:]
    planes = labels.shape[0]
    first = pltpu.make_async_copy(labels, label, sems.at[0])
    second = pltpu.make_async_copy(near_field, field, sems.at[1])
    first.start()
    second.start()
    others = []
    for n in range(3):
        others.append(pltpu.make_async_copy(sources[n], targets[n], sems.at[2 + n]))
        others[n].start()
    first.wait()
    for part in range(planes // halo):
        here = pl.ds(part * halo, halo)
        known = label[here]
        value = jnp.zeros(known.shape, jnp.float32)
        for region in range(table.shape[0]):
            value = jnp.where(known == region, table[region], value)
        rate[here] = value
    second.wait()
    near, far = edge_spots(planes)
    near_edge[...] = rate[pl.ds(near, halo)] * field[pl.ds(near, halo)]
    far_edge[...] = rate[pl.ds(far, halo)] * field[pl.ds(far, halo)]
    for copy in others:
        copy.wait()


def receivers_kernel(index, values, _, injected):
    steps, planes, nz, ny = injected.shape
    count = index.shape[1]
    local = index[0:1, :] - lax.axis_index("dom") * planes
    cell = jnp.where((local >= 0) & (local < planes), local * nz + index[1:2, :], -1)
    at_y = lax.broadcasted_iota(jnp.int32, (ny, count), 0) == index[2:3, :]
    parts = []
    for step in range(steps):
        for piece in pieces(values[step : step + 1, :]):
            spread = jnp.where(at_y, piece.astype(jnp.float32), 0.0)
            parts.append(spread.astype(jnp.bfloat16))
    group = halo
    rows = group * nz
    for part in range(planes // group):
        at_cell = lax.broadcasted_iota(jnp.int32, (rows, count), 0) + part * rows == cell
        picked = jnp.where(at_cell, 1.0, 0.0).astype(jnp.bfloat16)
        for step in range(steps):
            total = None
            for piece in reversed(parts[3 * step : 3 * step + 3]):
                term = lax.dot_general(
                    picked, piece, (((1,), (1,)), ((), ())), preferred_element_type=jnp.float32
                )
                total = term if total is None else total + term
            injected[step, pl.ds(part * group, group)] = total.reshape(group, nz, ny)


def forward_kernel(step, source, wavelet, *refs):
    current, previous, far, near, rate, _, upcoming, lap, near_edge, far_edge, ext = refs
    planes = current.shape[0]
    place(ext, near, far)
    ext[pl.ds(halo, planes)] = current[...]
    along_y, along_z = bands(current)
    for first in range(0, planes, halo):
        here = pl.ds(first, halo)
        value = laplacian(ext, first + halo, along_y, along_z)
        lap[here] = value
        upcoming[here] = 2.0 * current[here] - previous[here] + rate[here] * value
    add_source(upcoming, 0, planes, source, wavelet[0, step])
    near_at, far_at = edge_spots(planes)
    near_edge[...] = upcoming[pl.ds(near_at, halo)]
    far_edge[...] = upcoming[pl.ds(far_at, halo)]


def adjoint_kernel(step, *refs):
    current, later, near, far, rate, injected, earlier, near_edge, far_edge, ext = refs
    planes = current.shape[0]
    place(ext, near, far)
    ext[pl.ds(halo, planes)] = rate[...] * current[...]
    along_y, along_z = bands(current)
    for first in range(0, planes, halo):
        here = pl.ds(first, halo)
        value = laplacian(ext, first + halo, along_y, along_z)
        earlier[here] = 2.0 * current[here] - later[here] + value + injected[step, here]
    near_at, far_at = edge_spots(planes)
    near_edge[...] = rate[pl.ds(near_at, halo)] * earlier[pl.ds(near_at, halo)]
    far_edge[...] = rate[pl.ds(far_at, halo)] * earlier[pl.ds(far_at, halo)]


def turn_kernel(forward_step, step, source, wavelet, *refs):
    (current, later, near, far, rate, injected, lap1, lap2, lap3, wave, before, a5,
     earlier, near_edge, far_edge, rest, keep, send, inner, ext, grad) = refs
    planes = current.shape[0]
    place(ext, near, far)
    ext[pl.ds(halo, planes)] = rate[...] * current[...]
    along_y, along_z = bands(current)
    for first in range(0, planes, halo):
        here = pl.ds(first, halo)
        value = laplacian(ext, first + halo, along_y, along_z)
        value = 2.0 * current[here] - later[here] + value + injected[step, here]
        earlier[here] = value
        partial = later[here] * lap3[here] + current[here] * lap2[here] + value * lap1[here]
        if first == 0:
            rest[0] = partial
        elif first == planes - halo:
            rest[1] = partial
        else:
            value = laplacian(wave, first, along_y, along_z)
            within = pl.ds(first - halo, halo)
            inner[within] = 2.0 * wave[here] - before[here] + rate[here] * value
            grad[within] = partial + a5[here] * value
    add_source(inner, halo, planes, source, wavelet[0, forward_step])
    near_at, far_at = edge_spots(planes)
    near_edge[...] = rate[pl.ds(near_at, halo)] * earlier[pl.ds(near_at, halo)]
    far_edge[...] = rate[pl.ds(far_at, halo)] * earlier[pl.ds(far_at, halo)]
    half = keep.shape[0]
    mine = core() * half
    keep[...] = grad[pl.ds(mine, half)]
    send[...] = grad[pl.ds(half - mine, half)]


def forward_outer_kernel(step, source, wavelet, *refs):
    current, previous, far, near, rate, rest, a5, keep, send, outer, ext, grad = refs
    planes = current.shape[0]
    place(ext, near, far)
    ext[pl.ds(halo, planes)] = current[...]
    along_y, along_z = bands(current)
    for side, first in enumerate((0, planes - halo)):
        here = pl.ds(first, halo)
        value = laplacian(ext, first + halo, along_y, along_z)
        outer[side] = 2.0 * current[here] - previous[here] + rate[here] * value
        grad[side] = rest[side] + a5[here] * value
        add_source(outer.at[side], first, planes, source, wavelet[0, step])
    keep[...] = grad[core()]
    send[...] = grad[1 - core()]


def adjoint_inner_kernel(step, *refs):
    (current, later, rate, injected, inner, near_in, far_in, _,
     first_adjoint, final, near_edge, far_edge, ext, stage, sems) = refs
    planes = current.shape[0]
    within = pl.ds(halo, planes - 2 * halo)
    near_edge[...] = near_in[...]
    far_edge[...] = far_in[...]
    wave_copy = pltpu.make_async_copy(inner, final.at[within], sems.at[0])
    wave_copy.start()
    ext[...] = rate[...] * current[...]
    along_y, along_z = bands(current)
    for first in range(halo, planes - halo, halo):
        here = pl.ds(first, halo)
        value = laplacian(ext, first, along_y, along_z)
        stage[pl.ds(first - halo, halo)] = (
            2.0 * current[here] - later[here] + value + injected[step, here]
        )
    copy = pltpu.make_async_copy(stage, first_adjoint.at[within], sems.at[1])
    copy.start()
    wave_copy.wait()
    copy.wait()


def adjoint_outer_kernel(step, *refs):
    (current, later, near, far, rate, injected, outer_wave, _,
     outer, final, ext, sems) = refs
    planes = current.shape[0]
    copies = []
    for side, first in enumerate((0, planes - halo)):
        copies.append(
            pltpu.make_async_copy(
                outer_wave.at[side], final.at[pl.ds(first, halo)], sems.at[side]
            )
        )
        copies[side].start()
    place(ext, near, far)
    ext[pl.ds(halo, planes)] = rate[...] * current[...]
    along_y, along_z = bands(current)
    for side, first in enumerate((0, planes - halo)):
        here = pl.ds(first, halo)
        value = laplacian(ext, first + halo, along_y, along_z)
        outer[side] = 2.0 * current[here] - later[here] + value + injected[step, here]
    for copy in copies:
        copy.wait()


def finish_kernel(inner_kept, inner_got, kept, got, outer, _, first_adjoint, total, sems):
    planes = total.shape[0]
    half = inner_kept.shape[0]
    mine = core() * half
    side = core() * (planes - halo)
    spots = (
        (inner_kept, total, halo + mine, half),
        (inner_got, total, halo + half - mine, half),
        (kept, total, side, halo),
        (got, total, planes - halo - side, halo),
        (outer.at[0], first_adjoint, 0, halo),
        (outer.at[1], first_adjoint, planes - halo, halo),
    )
    copies = []
    for n, (piece, target, at, count) in enumerate(spots):
        copies.append(pltpu.make_async_copy(piece, target.at[pl.ds(at, count)], sems.at[n]))
        copies[n].start()
    for copy in copies:
        copy.wait()


def swap(near_edge, far_edge):
    count = lax.axis_size("dom")
    near_pairs = [(i, i ^ 1) for i in range(count) if i ^ 1 < count]
    far_pairs = [(i, i + 1) for i in range(1, count - 1, 2)]
    far_pairs = far_pairs + [(b, a) for a, b in far_pairs]
    far = lax.ppermute(far_edge, "dom", far_pairs)
    return lax.ppermute(near_edge, "dom", near_pairs), far


def parts_kernel(keep, *refs):
    parts, total = refs[:-2], refs[-1]
    size = parts[0].shape[0]
    for n, part in enumerate(parts):
        here = pl.ds(n * size, size)
        total[here] = keep[here] + part[...]


def add_kernel(a, b, _, total):
    total[...] = a[...] + b[...]


def first_sum(keep, send, after, count):
    shots = lax.axis_size("shot")
    pairs = [(i, i ^ 1) for i in range(shots)]
    across = [(i, i ^ 2) for i in range(shots)]
    size = send.shape[0] // count
    got = [lax.ppermute(send[n * size : (n + 1) * size], "shot", pairs) for n in range(count)]
    (kept,) = call(
        parts_kernel,
        (keep, *got, after),
        [vmem] * (1 + count) + [wherever],
        [(jax.ShapeDtypeStruct(keep.shape, jnp.float32), vmem)],
    )
    return kept, lax.ppermute(kept, "shot", across)


def second_sum(kept, got, after):
    shots = lax.axis_size("shot")
    pairs = [(i, i ^ 1) for i in range(shots)]
    (kept,) = call(
        add_kernel,
        (kept, got, after),
        [vmem, vmem, wherever],
        [(jax.ShapeDtypeStruct(kept.shape, jnp.float32), vmem)],
    )
    return kept, lax.ppermute(kept, "shot", pairs)


def per_device(
    wave_before,
    wave_current,
    adjoint_far,
    adjoint_near,
    labels,
    table,
    source_index,
    wavelet,
    receiver_index,
    residual,
):
    planes, nz, ny = wave_current.shape[1:]
    steps = wavelet.shape[1]
    odd = lax.axis_index("dom") % 2
    u0, u1 = wave_before[0], wave_current[0]
    a6, a5 = adjoint_far[0], adjoint_near[0]
    u0, u1, a6, a5, labels = (
        pltpu.with_memory_space_constraint(x, pltpu.HBM) for x in (u0, u1, a6, a5, labels)
    )
    whole = f32(planes, nz, ny)
    block = (whole, vmem)
    edge = (f32(halo, nz, ny), vmem)
    inner = planes - 2 * halo
    quarter = (f32(inner // 2, nz, ny), vmem)
    pair = (f32(2, halo, nz, ny), vmem)
    ext = pltpu.VMEM((planes + 2 * halo, nz, ny), jnp.float32)
    within = pltpu.VMEM((inner, nz, ny), jnp.float32)
    outer = pltpu.VMEM((2, halo, nz, ny), jnp.float32)

    near_at = jnp.where(odd == 1, 0, planes - halo)
    near_edge = lax.dynamic_slice_in_dim(wave_current[0], near_at, halo, axis=0)
    far_edge = lax.dynamic_slice_in_dim(wave_current[0], planes - halo - near_at, halo, axis=0)
    u_halo = swap(near_edge, far_edge)

    rate, near_edge, far_edge, a5, u1, u0, a6 = call(
        prepare_kernel,
        (table, labels, a5, u1, u0, a6),
        [vmem] + [hbm] * 5,
        [block, edge, edge] + [block] * 4,
        [pltpu.VMEM((planes, nz, ny), jnp.int32), pltpu.SemaphoreType.DMA((5,))],
    )
    a_halo = swap(near_edge, far_edge)

    (injected,) = call(
        receivers_kernel,
        (receiver_index[0].T, residual[0], rate),
        [vmem, vmem, wherever],
        [(f32(steps, planes, nz, ny), vmem)],
    )

    laps = []
    previous, current = u0, u1
    later, adjoint = a6, a5
    for n in range(steps - 1):
        upcoming, lap, near_edge, far_edge = call(
            functools.partial(forward_kernel, n),
            (source_index, wavelet, current, previous, *u_halo[::-1], rate, injected),
            [vmem] * 7 + [wherever],
            [block, block, edge, edge],
            [ext],
        )
        laps.append(lap)
        u_halo = swap(near_edge, far_edge)
        previous, current = current, upcoming
        step = steps - 1 - n
        if n < steps - 2:
            earlier, near_edge, far_edge = call(
                functools.partial(adjoint_kernel, step),
                (adjoint, later, *a_halo, rate, injected),
                [vmem] * 6,
                [block, edge, edge],
                [ext],
            )
        else:
            earlier, near_edge, far_edge, rest, keep, send, inner_wave = call(
                functools.partial(turn_kernel, steps - 1, step),
                (source_index, wavelet, adjoint, later, *a_halo, rate, injected, *laps,
                 current, previous, a5),
                [vmem] * 14,
                [block, edge, edge, pair, quarter, quarter, (f32(inner, nz, ny), vmem)],
                [ext, within],
            )
        if n < steps - 2:
            a_halo = swap(near_edge, far_edge)
        later, adjoint = adjoint, earlier

    inner_sum = first_sum(keep, send, keep, 4)
    first_adjoint, final, near_edge, far_edge = call(
        functools.partial(adjoint_inner_kernel, 0),
        (adjoint, later, rate, injected, inner_wave, near_edge, far_edge, inner_sum[0]),
        [vmem] * 7 + [wherever],
        [(whole, hbm), (whole, hbm), edge, edge],
        [pltpu.VMEM((planes, nz, ny), jnp.float32), within, pltpu.SemaphoreType.DMA((2,))],
    )
    a_halo = swap(near_edge, far_edge)
    keep, send, outer_wave = call(
        functools.partial(forward_outer_kernel, steps - 1),
        (source_index, wavelet, current, previous, *u_halo[::-1], rate, rest, a5),
        [vmem] * 9,
        [edge, edge, pair],
        [ext, outer],
    )
    outer_sum = first_sum(keep, send, inner_sum[1], 2)
    last_outer, final = call(
        functools.partial(adjoint_outer_kernel, 0),
        (adjoint, later, *a_halo, rate, injected, outer_wave, final),
        [vmem] * 7 + [hbm],
        [pair, (whole, hbm)],
        [ext, pltpu.SemaphoreType.DMA((2,))],
        {7: 1},
        cost=2000000000,
    )
    inner_kept, inner_got = second_sum(*inner_sum, last_outer)
    kept, got = second_sum(*outer_sum, last_outer)
    first_adjoint, total = call(
        finish_kernel,
        (inner_kept, inner_got, kept, got, last_outer, first_adjoint),
        [vmem] * 5 + [hbm],
        [(whole, hbm), (whole, hbm)],
        [pltpu.SemaphoreType.DMA((6,))],
        {5: 0},
    )
    return (final[None], first_adjoint[None], total)


def solution(mesh):
    placed = (
        P("shot", "dom", None, None),
        P("shot", "dom", None, None),
        P("shot", "dom", None, None),
        P("shot", "dom", None, None),
        P("dom", None, None),
        P(),
        P("shot", None),
        P("shot", None),
        P("shot", None, None),
        P("shot", None, None),
    )
    return jax.shard_map(
        per_device,
        mesh=mesh,
        in_specs=placed,
        out_specs=(
            P("shot", "dom", None, None),
            P("shot", "dom", None, None),
            P("dom", None, None),
        ),
        check_vma=False,
    )
```

```python
import functools

import jax
import jax.numpy as jnp
from jax import lax
from jax.experimental import pallas as pl
from jax.experimental.pallas import tpu as pltpu
from jax.sharding import PartitionSpec as P

centre_coef = -205.0 / 72.0
side_coefs = (8.0 / 5.0, -1.0 / 5.0, 8.0 / 315.0, -1.0 / 560.0)
unit = 5040.0
side_units = (8064.0, -1008.0, 128.0, -9.0)
halo = 4

vmem = pl.BlockSpec(memory_space=pltpu.VMEM)
hbm = pl.BlockSpec(memory_space=pltpu.HBM)
wherever = pl.BlockSpec(memory_space=pl.ANY)


def call(kernel, args, in_specs, outs, scratch=(), aliases={}, limit=24, cost=1024):
    return pl.pallas_call(
        kernel,
        out_shape=[
            pltpu.VMEM(shape.shape, shape.dtype) if spec is vmem else shape for shape, spec in outs
        ],
        in_specs=in_specs,
        out_specs=[spec for _, spec in outs],
        scratch_shapes=list(scratch),
        input_output_aliases=aliases,
        compiler_params=pltpu.CompilerParams(vmem_limit_bytes=limit * 1024 * 1024),
        cost_estimate=pl.CostEstimate(flops=cost, bytes_accessed=1024, transcendentals=0),
    )(*args)


def f32(*shape):
    return jax.ShapeDtypeStruct(shape, jnp.float32)


def band(size, block):
    row = lax.broadcasted_iota(jnp.int32, (size, size), 0)
    col = lax.broadcasted_iota(jnp.int32, (size, size), 1)
    apart = jnp.abs(row - col)
    value = jnp.zeros((size, size), jnp.float32)
    for k in range(1, 5):
        value = jnp.where(apart == k, side_units[k - 1], value)
    if block != size:
        value = jnp.where(lax.div(row, block) == lax.div(col, block), value, 0.0)
    return value.astype(jnp.bfloat16)


def pieces(value):
    high = value.astype(jnp.bfloat16)
    rest = value - high.astype(jnp.float32)
    middle = rest.astype(jnp.bfloat16)
    low = (rest - middle.astype(jnp.float32)).astype(jnp.bfloat16)
    return high, middle, low


def dot(a, b):
    return lax.dot_general(a, b, (((1,), (0,)), ((), ())), preferred_element_type=jnp.float32)


def laplacian(field, at, along_y, along_z):
    _, nz, ny = field.shape
    along_y, along_z = along_y[...], along_z[...]
    centre = field[pl.ds(at, halo)]
    high, middle, low = pieces(centre.reshape(halo * nz, ny))
    across = dot(low, along_y) + dot(along_z, low)
    across = across + (dot(middle, along_y) + dot(along_z, middle))
    across = across + (dot(high, along_y) + dot(along_z, high))
    result = 3.0 * centre_coef * centre + across.reshape(halo, nz, ny) * (1.0 / unit)
    for k in range(1, 5):
        result = result + side_coefs[k - 1] * (
            field[pl.ds(at + k, halo)] + field[pl.ds(at - k, halo)]
        )
    return result


def beyond(sides, side):
    outside = sides[side]
    result = None
    for k in range(4, 0, -1):
        if side == 0:
            term = outside[halo - k : halo]
        else:
            term = outside[:k]
        term = side_coefs[k - 1] * term
        if k < halo:
            empty = jnp.zeros((halo - k,) + outside.shape[1:], jnp.float32)
            term = jnp.concatenate([term, empty] if side == 0 else [empty, term], axis=0)
        result = term if result is None else result + term
    return result


def core():
    return lax.axis_index("shot") % 2


def place(ext, near, far):
    planes = ext.shape[0] - 2 * halo
    odd = lax.axis_index("dom") % 2
    spot = jnp.where(odd == 1, 0, planes + halo)
    ext[pl.ds(spot, halo)] = near[...]
    ext[pl.ds(planes + halo - spot, halo)] = far[...]


def place_sides(sides, near, far):
    odd = lax.axis_index("dom") % 2
    sides[1 - odd] = near[...]
    sides[odd] = far[...]


def alone(ext, block):
    planes = block.shape[0]
    empty = jnp.zeros((halo,) + block.shape[1:], jnp.float32)
    ext[pl.ds(0, halo)] = empty
    ext[pl.ds(planes + halo, halo)] = empty
    ext[pl.ds(halo, planes)] = block


def edge_spots(planes):
    odd = lax.axis_index("dom") % 2
    near = jnp.where(odd == 1, 0, planes - halo)
    return near, planes - halo - near


def add_source(field, first, planes, source, value):
    count, _, ny = field.shape
    x = source[0, 0] - lax.axis_index("dom") * planes - first
    z = source[0, 1]
    y = source[0, 2]

    @pl.when((x >= 0) & (x < count))
    def _():
        base = pl.multiple_of(lax.div(z, 8) * 8, 8)
        rows = lax.broadcasted_iota(jnp.int32, (8, ny), 0)
        cols = lax.broadcasted_iota(jnp.int32, (8, ny), 1)
        hit = (rows == z - base) & (cols == y)
        tile = field[x, pl.ds(base, 8), :]
        field[x, pl.ds(base, 8), :] = tile + jnp.where(hit, value, 0.0)


def prepare_kernel(
    table, labels, near_field, *refs
):
    sources, refs = refs[:3], refs[3:]
    rate, near_edge, far_edge, along_y, along_z, field, *targets = refs[:9]
    label, sems = refs[9:]
    planes = labels.shape[0]
    first = pltpu.make_async_copy(labels, label, sems.at[0])
    second = pltpu.make_async_copy(near_field, field, sems.at[1])
    first.start()
    second.start()
    others = []
    for n in range(3):
        others.append(pltpu.make_async_copy(sources[n], targets[n], sems.at[2 + n]))
        others[n].start()
    _, nz, ny = labels.shape
    along_y[...] = band(ny, ny)
    along_z[...] = band(halo * nz, nz)
    first.wait()
    for part in range(planes // halo):
        here = pl.ds(part * halo, halo)
        known = label[here]
        value = jnp.zeros(known.shape, jnp.float32)
        for region in range(table.shape[0]):
            value = jnp.where(known == region, table[region], value)
        rate[here] = value
    second.wait()
    near, far = edge_spots(planes)
    near_edge[...] = rate[pl.ds(near, halo)] * field[pl.ds(near, halo)]
    far_edge[...] = rate[pl.ds(far, halo)] * field[pl.ds(far, halo)]
    for copy in others:
        copy.wait()


def receivers_kernel(index, values, _, injected):
    steps, planes, nz, ny = injected.shape
    count = index.shape[1]
    local = index[0:1, :] - lax.axis_index("dom") * planes
    cell = jnp.where((local >= 0) & (local < planes), local * nz + index[1:2, :], -1)
    at_y = lax.broadcasted_iota(jnp.int32, (ny, count), 0) == index[2:3, :]
    parts = []
    for step in range(steps):
        for piece in pieces(values[step : step + 1, :]):
            spread = jnp.where(at_y, piece.astype(jnp.float32), 0.0)
            parts.append(spread.astype(jnp.bfloat16))
    group = halo
    rows = group * nz
    for part in range(planes // group):
        at_cell = lax.broadcasted_iota(jnp.int32, (rows, count), 0) + part * rows == cell
        picked = jnp.where(at_cell, 1.0, 0.0).astype(jnp.bfloat16)
        for step in range(steps):
            total = None
            for piece in reversed(parts[3 * step : 3 * step + 3]):
                term = lax.dot_general(
                    picked, piece, (((1,), (1,)), ((), ())), preferred_element_type=jnp.float32
                )
                total = term if total is None else total + term
            injected[step, pl.ds(part * group, group)] = total.reshape(group, nz, ny)


def forward_kernel(step, *refs):
    *bands, source, wavelet = refs[:4]
    refs = refs[4:]
    current, previous, far, near, rate, _, upcoming, lap, near_edge, far_edge, ext = refs
    planes = current.shape[0]
    place(ext, near, far)
    ext[pl.ds(halo, planes)] = current[...]
    for first in range(0, planes, halo):
        here = pl.ds(first, halo)
        value = laplacian(ext, first + halo, *bands)
        lap[here] = value
        upcoming[here] = 2.0 * current[here] - previous[here] + rate[here] * value
    add_source(upcoming, 0, planes, source, wavelet[0, step])
    near_at, far_at = edge_spots(planes)
    near_edge[...] = upcoming[pl.ds(near_at, halo)]
    far_edge[...] = upcoming[pl.ds(far_at, halo)]


def adjoint_kernel(step, *refs):
    bands, refs = refs[:2], refs[2:]
    current, later, near, far, rate, injected, earlier, near_edge, far_edge, ext = refs
    planes = current.shape[0]
    place(ext, near, far)
    ext[pl.ds(halo, planes)] = rate[...] * current[...]
    for first in range(0, planes, halo):
        here = pl.ds(first, halo)
        value = laplacian(ext, first + halo, *bands)
        earlier[here] = 2.0 * current[here] - later[here] + value + injected[step, here]
    near_at, far_at = edge_spots(planes)
    near_edge[...] = rate[pl.ds(near_at, halo)] * earlier[pl.ds(near_at, halo)]
    far_edge[...] = rate[pl.ds(far_at, halo)] * earlier[pl.ds(far_at, halo)]


def turn_kernel(forward_step, step, *refs):
    *bands, source, wavelet = refs[:4]
    refs = refs[4:]
    (current, later, near, far, rate, injected, lap1, lap2, lap3, wave, before, a5,
     earlier, near_edge, far_edge, rest, part, keep, send, inner, ext, wide, grad) = refs
    planes = current.shape[0]
    place(ext, near, far)
    ext[pl.ds(halo, planes)] = rate[...] * current[...]
    alone(wide, wave[...])
    for first in range(0, planes, halo):
        here = pl.ds(first, halo)
        value = laplacian(ext, first + halo, *bands)
        value = 2.0 * current[here] - later[here] + value + injected[step, here]
        earlier[here] = value
        partial = later[here] * lap3[here] + current[here] * lap2[here] + value * lap1[here]
        value = laplacian(wide, first + halo, *bands)
        partial = partial + a5[here] * value
        value = 2.0 * wave[here] - before[here] + rate[here] * value
        if first == 0 or first == planes - halo:
            side = 0 if first == 0 else 1
            rest[side] = partial
            part[side] = value
        else:
            within = pl.ds(first - halo, halo)
            inner[within] = value
            grad[within] = partial
    for side, first in enumerate((0, planes - halo)):
        add_source(part.at[side], first, planes, source, wavelet[0, forward_step])
    add_source(inner, halo, planes, source, wavelet[0, forward_step])
    near_at, far_at = edge_spots(planes)
    near_edge[...] = rate[pl.ds(near_at, halo)] * earlier[pl.ds(near_at, halo)]
    far_edge[...] = rate[pl.ds(far_at, halo)] * earlier[pl.ds(far_at, halo)]
    half = keep.shape[0]
    mine = core() * half
    keep[...] = grad[pl.ds(mine, half)]
    send[...] = grad[pl.ds(half - mine, half)]


def forward_outer_kernel(far, near, rate, part, rest, a5, keep, send, outer, sides, grad):
    planes = rate.shape[0]
    place_sides(sides, near, far)
    for side, first in enumerate((0, planes - halo)):
        here = pl.ds(first, halo)
        value = beyond(sides, side)
        outer[side] = part[side] + rate[here] * value
        grad[side] = rest[side] + a5[here] * value
    keep[...] = grad[core()]
    send[...] = grad[1 - core()]


def pass_kernel(near, far, _, near_edge, far_edge):
    near_edge[...] = near[...]
    far_edge[...] = far[...]


def adjoint_inner_kernel(step, *refs):
    (*bands, current, later, rate, injected, inner, outer,
     first_adjoint, final, part, ext, stage, sems) = refs
    planes = current.shape[0]
    edge = planes - halo
    copies = []
    for piece, low, high in ((inner, halo, edge), (outer.at[0], 0, halo), (outer.at[1], edge, planes)):
        copies.append(pltpu.make_async_copy(piece, final.at[low:high], sems.at[len(copies)]))
        copies[-1].start()
    alone(ext, rate[...] * current[...])
    for first in range(0, planes, halo):
        here = pl.ds(first, halo)
        value = laplacian(ext, first + halo, *bands)
        value = 2.0 * current[here] - later[here] + value + injected[step, here]
        if first == 0 or first == edge:
            part[0 if first == 0 else 1] = value
        else:
            stage[pl.ds(first - halo, halo)] = value
    copies.append(pltpu.make_async_copy(stage, first_adjoint.at[halo:edge], sems.at[3]))
    copies[-1].start()
    for copy in copies:
        copy.wait()


def adjoint_outer_kernel(near, far, part, outer, sides):
    place_sides(sides, near, far)
    for side in range(2):
        outer[side] = part[side] + beyond(sides, side)


def finish_kernel(inner_kept, inner_got, kept, got, outer, _, first_adjoint, total, sems):
    planes = total.shape[0]
    half = inner_kept.shape[0]
    mine = core() * half
    side = core() * (planes - halo)
    spots = (
        (inner_kept, total, halo + mine, half),
        (inner_got, total, halo + half - mine, half),
        (kept, total, side, halo),
        (got, total, planes - halo - side, halo),
        (outer.at[0], first_adjoint, 0, halo),
        (outer.at[1], first_adjoint, planes - halo, halo),
    )
    copies = []
    for n, (piece, target, at, count) in enumerate(spots):
        copies.append(pltpu.make_async_copy(piece, target.at[pl.ds(at, count)], sems.at[n]))
        copies[n].start()
    for copy in copies:
        copy.wait()


def swap(near_edge, far_edge):
    count = lax.axis_size("dom")
    near_pairs = [(i, i ^ 1) for i in range(count) if i ^ 1 < count]
    far_pairs = [(i, i + 1) for i in range(1, count - 1, 2)]
    far_pairs = far_pairs + [(b, a) for a, b in far_pairs]
    far = lax.ppermute(far_edge, "dom", far_pairs)
    return lax.ppermute(near_edge, "dom", near_pairs), far


def parts_kernel(keep, *refs):
    parts, total = refs[:-2], refs[-1]
    size = parts[0].shape[0]
    for n, part in enumerate(parts):
        here = pl.ds(n * size, size)
        total[here] = keep[here] + part[...]


def add_kernel(a, b, _, total):
    total[...] = a[...] + b[...]


def first_sum(keep, send, after, count):
    shots = lax.axis_size("shot")
    pairs = [(i, i ^ 1) for i in range(shots)]
    across = [(i, i ^ 2) for i in range(shots)]
    size = send.shape[0] // count
    got = [lax.ppermute(send[n * size : (n + 1) * size], "shot", pairs) for n in range(count)]
    (kept,) = call(
        parts_kernel,
        (keep, *got, after),
        [vmem] * (1 + count) + [wherever],
        [(jax.ShapeDtypeStruct(keep.shape, jnp.float32), vmem)],
    )
    return kept, lax.ppermute(kept, "shot", across)


def second_sum(kept, got, after):
    shots = lax.axis_size("shot")
    pairs = [(i, i ^ 1) for i in range(shots)]
    (kept,) = call(
        add_kernel,
        (kept, got, after),
        [vmem, vmem, wherever],
        [(jax.ShapeDtypeStruct(kept.shape, jnp.float32), vmem)],
    )
    return kept, lax.ppermute(kept, "shot", pairs)


def per_device(
    wave_before,
    wave_current,
    adjoint_far,
    adjoint_near,
    labels,
    table,
    source_index,
    wavelet,
    receiver_index,
    residual,
):
    planes, nz, ny = wave_current.shape[1:]
    steps = wavelet.shape[1]
    odd = lax.axis_index("dom") % 2
    u0, u1 = wave_before[0], wave_current[0]
    a6, a5 = adjoint_far[0], adjoint_near[0]
    u0, u1, a6, a5, labels = (
        pltpu.with_memory_space_constraint(x, pltpu.HBM) for x in (u0, u1, a6, a5, labels)
    )
    whole = f32(planes, nz, ny)
    block = (whole, vmem)
    edge = (f32(halo, nz, ny), vmem)
    inner = planes - 2 * halo
    quarter = (f32(inner // 2, nz, ny), vmem)
    pair = (f32(2, halo, nz, ny), vmem)
    ext = pltpu.VMEM((planes + 2 * halo, nz, ny), jnp.float32)
    within = pltpu.VMEM((inner, nz, ny), jnp.float32)

    near_at = jnp.where(odd == 1, 0, planes - halo)
    near_edge = lax.dynamic_slice_in_dim(wave_current[0], near_at, halo, axis=0)
    far_edge = lax.dynamic_slice_in_dim(wave_current[0], planes - halo - near_at, halo, axis=0)
    u_halo = swap(near_edge, far_edge)

    rate, near_edge, far_edge, *bands, a5, u1, u0, a6 = call(
        prepare_kernel,
        (table, labels, a5, u1, u0, a6),
        [vmem] + [hbm] * 5,
        [block, edge, edge]
        + [(jax.ShapeDtypeStruct((n, n), jnp.bfloat16), vmem) for n in (ny, halo * nz)]
        + [block] * 4,
        [pltpu.VMEM((planes, nz, ny), jnp.int32), pltpu.SemaphoreType.DMA((5,))],
    )
    a_halo = swap(near_edge, far_edge)

    (injected,) = call(
        receivers_kernel,
        (receiver_index[0].T, residual[0], rate),
        [vmem, vmem, wherever],
        [(f32(steps, planes, nz, ny), vmem)],
    )

    laps = []
    previous, current = u0, u1
    later, adjoint = a6, a5
    for n in range(steps - 1):
        upcoming, lap, near_edge, far_edge = call(
            functools.partial(forward_kernel, n),
            (*bands, source_index, wavelet, current, previous, *u_halo[::-1], rate, injected),
            [vmem] * 9 + [wherever],
            [block, block, edge, edge],
            [ext],
        )
        laps.append(lap)
        u_halo = swap(near_edge, far_edge)
        previous, current = current, upcoming
        step = steps - 1 - n
        if n < steps - 2:
            earlier, near_edge, far_edge = call(
                functools.partial(adjoint_kernel, step),
                (*bands, adjoint, later, *a_halo, rate, injected),
                [vmem] * 8,
                [block, edge, edge],
                [ext],
            )
        else:
            earlier, near_edge, far_edge, rest, part, keep, send, inner_wave = call(
                functools.partial(turn_kernel, steps - 1, step),
                (*bands, source_index, wavelet, adjoint, later, *a_halo, rate, injected, *laps,
                 current, previous, a5),
                [vmem] * 16,
                [block, edge, edge, pair, pair, quarter, quarter, (f32(inner, nz, ny), vmem)],
                [ext, ext, within],
            )
        if n < steps - 2:
            a_halo = swap(near_edge, far_edge)
        later, adjoint = adjoint, earlier

    inner_sum = first_sum(keep, send, keep, 4)
    near_edge, far_edge = call(
        pass_kernel,
        (near_edge, far_edge, inner_sum[0]),
        [vmem, vmem, wherever],
        [edge, edge],
    )
    a_halo = swap(near_edge, far_edge)
    outer = pltpu.VMEM((2, halo, nz, ny), jnp.float32)
    keep, send, outer_wave = call(
        forward_outer_kernel,
        (*u_halo[::-1], rate, part, rest, a5),
        [vmem] * 6,
        [edge, edge, pair],
        [outer, outer],
    )
    outer_sum = first_sum(keep, send, inner_sum[1], 2)
    first_adjoint, final, part = call(
        functools.partial(adjoint_inner_kernel, 0),
        (*bands, adjoint, later, rate, injected, inner_wave, outer_wave),
        [vmem] * 8,
        [(whole, hbm), (whole, hbm), pair],
        [ext, within, pltpu.SemaphoreType.DMA((4,))],
    )
    (last_outer,) = call(
        adjoint_outer_kernel,
        (*a_halo, part),
        [vmem] * 3,
        [pair],
        [outer],
        cost=2000000000,
    )
    inner_kept, inner_got = second_sum(*inner_sum, last_outer)
    kept, got = second_sum(*outer_sum, last_outer)
    first_adjoint, total = call(
        finish_kernel,
        (inner_kept, inner_got, kept, got, last_outer, first_adjoint),
        [vmem] * 5 + [hbm],
        [(whole, hbm), (whole, hbm)],
        [pltpu.SemaphoreType.DMA((6,))],
        {5: 0},
    )
    return (final[None], first_adjoint[None], total)


def solution(mesh):
    placed = (
        P("shot", "dom", None, None),
        P("shot", "dom", None, None),
        P("shot", "dom", None, None),
        P("shot", "dom", None, None),
        P("dom", None, None),
        P(),
        P("shot", None),
        P("shot", None),
        P("shot", None, None),
        P("shot", None, None),
    )
    return jax.shard_map(
        per_device,
        mesh=mesh,
        in_specs=placed,
        out_specs=(
            P("shot", "dom", None, None),
            P("shot", "dom", None, None),
            P("dom", None, None),
        ),
        check_vma=False,
    )
```

```python
import functools

import jax
import jax.numpy as jnp
from jax import lax
from jax.experimental import pallas as pl
from jax.experimental.pallas import tpu as pltpu
from jax.sharding import PartitionSpec as P

centre_coef = -205.0 / 72.0
side_coefs = (8.0 / 5.0, -1.0 / 5.0, 8.0 / 315.0, -1.0 / 560.0)
unit = 5040.0
side_units = (8064.0, -1008.0, 128.0, -9.0)
halo = 4

vmem = pl.BlockSpec(memory_space=pltpu.VMEM)
hbm = pl.BlockSpec(memory_space=pltpu.HBM)
wherever = pl.BlockSpec(memory_space=pl.ANY)


def call(kernel, args, in_specs, outs, scratch=(), aliases={}, limit=24, cost=1024):
    return pl.pallas_call(
        kernel,
        out_shape=[
            pltpu.VMEM(shape.shape, shape.dtype) if spec is vmem else shape for shape, spec in outs
        ],
        in_specs=in_specs,
        out_specs=[spec for _, spec in outs],
        scratch_shapes=list(scratch),
        input_output_aliases=aliases,
        compiler_params=pltpu.CompilerParams(vmem_limit_bytes=limit * 1024 * 1024),
        cost_estimate=pl.CostEstimate(flops=cost, bytes_accessed=1024, transcendentals=0),
    )(*args)


def f32(*shape):
    return jax.ShapeDtypeStruct(shape, jnp.float32)


def band(size, block):
    row = lax.broadcasted_iota(jnp.int32, (size, size), 0)
    col = lax.broadcasted_iota(jnp.int32, (size, size), 1)
    apart = jnp.abs(row - col)
    value = jnp.zeros((size, size), jnp.float32)
    for k in range(1, 5):
        value = jnp.where(apart == k, side_units[k - 1], value)
    if block != size:
        value = jnp.where(lax.div(row, block) == lax.div(col, block), value, 0.0)
    return value.astype(jnp.bfloat16)


def pieces(value):
    high = value.astype(jnp.bfloat16)
    rest = value - high.astype(jnp.float32)
    middle = rest.astype(jnp.bfloat16)
    low = (rest - middle.astype(jnp.float32)).astype(jnp.bfloat16)
    return high, middle, low


def dot(a, b):
    return lax.dot_general(a, b, (((1,), (0,)), ((), ())), preferred_element_type=jnp.float32)


def laplacian(field, at, along_y, along_z):
    _, nz, ny = field.shape
    along_y, along_z = along_y[...], along_z[...]
    centre = field[pl.ds(at, halo)]
    high, middle, low = pieces(centre.reshape(halo * nz, ny))
    across = dot(low, along_y) + dot(along_z, low)
    across = across + (dot(middle, along_y) + dot(along_z, middle))
    across = across + (dot(high, along_y) + dot(along_z, high))
    result = 3.0 * centre_coef * centre + across.reshape(halo, nz, ny) * (1.0 / unit)
    for k in range(1, 5):
        result = result + side_coefs[k - 1] * (
            field[pl.ds(at + k, halo)] + field[pl.ds(at - k, halo)]
        )
    return result


def beyond(sides, side):
    outside = sides[side]
    result = None
    for k in range(4, 0, -1):
        if side == 0:
            term = outside[halo - k : halo]
        else:
            term = outside[:k]
        term = side_coefs[k - 1] * term
        if k < halo:
            empty = jnp.zeros((halo - k,) + outside.shape[1:], jnp.float32)
            term = jnp.concatenate([term, empty] if side == 0 else [empty, term], axis=0)
        result = term if result is None else result + term
    return result


def core():
    return lax.axis_index("shot") % 2


def place(ext, near, far):
    planes = ext.shape[0] - 2 * halo
    odd = lax.axis_index("dom") % 2
    spot = jnp.where(odd == 1, 0, planes + halo)
    ext[pl.ds(spot, halo)] = near[...]
    ext[pl.ds(planes + halo - spot, halo)] = far[...]


def place_sides(sides, near, far):
    odd = lax.axis_index("dom") % 2
    sides[1 - odd] = near[...]
    sides[odd] = far[...]


def alone(ext, block):
    planes = block.shape[0]
    empty = jnp.zeros((halo,) + block.shape[1:], jnp.float32)
    ext[pl.ds(0, halo)] = empty
    ext[pl.ds(planes + halo, halo)] = empty
    ext[pl.ds(halo, planes)] = block


def edge_spots(planes):
    odd = lax.axis_index("dom") % 2
    near = jnp.where(odd == 1, 0, planes - halo)
    return near, planes - halo - near


def add_source(field, first, planes, source, value):
    count, _, ny = field.shape
    x = source[0, 0] - lax.axis_index("dom") * planes - first
    z = source[0, 1]
    y = source[0, 2]

    @pl.when((x >= 0) & (x < count))
    def _():
        base = pl.multiple_of(lax.div(z, 8) * 8, 8)
        rows = lax.broadcasted_iota(jnp.int32, (8, ny), 0)
        cols = lax.broadcasted_iota(jnp.int32, (8, ny), 1)
        hit = (rows == z - base) & (cols == y)
        tile = field[x, pl.ds(base, 8), :]
        field[x, pl.ds(base, 8), :] = tile + jnp.where(hit, value, 0.0)


def prepare_kernel(
    table, labels, near_field, *refs
):
    sources, refs = refs[:3], refs[3:]
    rate, near_edge, far_edge, along_y, along_z, field, *targets = refs[:9]
    label, sems = refs[9:]
    planes = labels.shape[0]
    first = pltpu.make_async_copy(labels, label, sems.at[0])
    second = pltpu.make_async_copy(near_field, field, sems.at[1])
    first.start()
    second.start()
    others = []
    for n in range(3):
        others.append(pltpu.make_async_copy(sources[n], targets[n], sems.at[2 + n]))
        others[n].start()
    _, nz, ny = labels.shape
    along_y[...] = band(ny, ny)
    along_z[...] = band(halo * nz, nz)
    first.wait()
    for part in range(planes // halo):
        here = pl.ds(part * halo, halo)
        known = label[here]
        value = jnp.zeros(known.shape, jnp.float32)
        for region in range(table.shape[0]):
            value = jnp.where(known == region, table[region], value)
        rate[here] = value
    second.wait()
    near, far = edge_spots(planes)
    near_edge[...] = rate[pl.ds(near, halo)] * field[pl.ds(near, halo)]
    far_edge[...] = rate[pl.ds(far, halo)] * field[pl.ds(far, halo)]
    for copy in others:
        copy.wait()


def receivers_kernel(index, values, _, injected):
    steps, planes, nz, ny = injected.shape
    count = index.shape[1]
    local = index[0:1, :] - lax.axis_index("dom") * planes
    cell = jnp.where((local >= 0) & (local < planes), local * nz + index[1:2, :], -1)
    at_y = lax.broadcasted_iota(jnp.int32, (ny, count), 0) == index[2:3, :]
    parts = []
    for step in range(steps):
        for piece in pieces(values[step : step + 1, :]):
            spread = jnp.where(at_y, piece.astype(jnp.float32), 0.0)
            parts.append(spread.astype(jnp.bfloat16))
    group = halo
    rows = group * nz
    for part in range(planes // group):
        at_cell = lax.broadcasted_iota(jnp.int32, (rows, count), 0) + part * rows == cell
        picked = jnp.where(at_cell, 1.0, 0.0).astype(jnp.bfloat16)
        for step in range(steps):
            total = None
            for piece in reversed(parts[3 * step : 3 * step + 3]):
                term = lax.dot_general(
                    picked, piece, (((1,), (1,)), ((), ())), preferred_element_type=jnp.float32
                )
                total = term if total is None else total + term
            injected[step, pl.ds(part * group, group)] = total.reshape(group, nz, ny)


def forward_kernel(step, *refs):
    *bands, source, wavelet = refs[:4]
    refs = refs[4:]
    current, previous, far, near, rate, _, upcoming, lap, near_edge, far_edge, ext = refs
    planes = current.shape[0]
    place(ext, near, far)
    ext[pl.ds(halo, planes)] = current[...]
    for first in range(0, planes, halo):
        here = pl.ds(first, halo)
        value = laplacian(ext, first + halo, *bands)
        lap[here] = value
        upcoming[here] = 2.0 * current[here] - previous[here] + rate[here] * value
    add_source(upcoming, 0, planes, source, wavelet[0, step])
    near_at, far_at = edge_spots(planes)
    near_edge[...] = upcoming[pl.ds(near_at, halo)]
    far_edge[...] = upcoming[pl.ds(far_at, halo)]


def adjoint_kernel(step, *refs):
    bands, refs = refs[:2], refs[2:]
    current, later, near, far, rate, injected, earlier, near_edge, far_edge, ext = refs
    planes = current.shape[0]
    place(ext, near, far)
    ext[pl.ds(halo, planes)] = rate[...] * current[...]
    for first in range(0, planes, halo):
        here = pl.ds(first, halo)
        value = laplacian(ext, first + halo, *bands)
        earlier[here] = 2.0 * current[here] - later[here] + value + injected[step, here]
    near_at, far_at = edge_spots(planes)
    near_edge[...] = rate[pl.ds(near_at, halo)] * earlier[pl.ds(near_at, halo)]
    far_edge[...] = rate[pl.ds(far_at, halo)] * earlier[pl.ds(far_at, halo)]


def turn_kernel(forward_step, step, *refs):
    *bands, source, wavelet = refs[:4]
    refs = refs[4:]
    (current, later, near, far, rate, injected, lap1, lap2, lap3, wave, before, a5,
     earlier, near_edge, far_edge, rest, part, keep, send, inner, ext, wide, grad) = refs
    planes = current.shape[0]
    place(ext, near, far)
    ext[pl.ds(halo, planes)] = rate[...] * current[...]
    alone(wide, wave[...])
    for first in range(0, planes, halo):
        here = pl.ds(first, halo)
        value = laplacian(ext, first + halo, *bands)
        value = 2.0 * current[here] - later[here] + value + injected[step, here]
        earlier[here] = value
        partial = later[here] * lap3[here] + current[here] * lap2[here] + value * lap1[here]
        value = laplacian(wide, first + halo, *bands)
        partial = partial + a5[here] * value
        value = 2.0 * wave[here] - before[here] + rate[here] * value
        if first == 0 or first == planes - halo:
            side = 0 if first == 0 else 1
            rest[side] = partial
            part[side] = value
        else:
            within = pl.ds(first - halo, halo)
            inner[within] = value
            grad[within] = partial
    for side, first in enumerate((0, planes - halo)):
        add_source(part.at[side], first, planes, source, wavelet[0, forward_step])
    add_source(inner, halo, planes, source, wavelet[0, forward_step])
    near_at, far_at = edge_spots(planes)
    near_edge[...] = rate[pl.ds(near_at, halo)] * earlier[pl.ds(near_at, halo)]
    far_edge[...] = rate[pl.ds(far_at, halo)] * earlier[pl.ds(far_at, halo)]
    half = keep.shape[0]
    mine = core() * half
    keep[...] = grad[pl.ds(mine, half)]
    send[...] = grad[pl.ds(half - mine, half)]


def forward_outer_kernel(far, near, rate, part, rest, a5, keep, send, outer, sides, grad):
    planes = rate.shape[0]
    place_sides(sides, near, far)
    for side, first in enumerate((0, planes - halo)):
        here = pl.ds(first, halo)
        value = beyond(sides, side)
        outer[side] = part[side] + rate[here] * value
        grad[side] = rest[side] + a5[here] * value
    keep[...] = grad[core()]
    send[...] = grad[1 - core()]


def pass_kernel(near, far, _, near_edge, far_edge):
    near_edge[...] = near[...]
    far_edge[...] = far[...]


def adjoint_inner_kernel(step, *refs):
    (*bands, current, later, rate, injected, inner, outer,
     first_adjoint, final, part, ext, stage, sems) = refs
    planes = current.shape[0]
    edge = planes - halo
    copies = []
    for piece, low, high in ((inner, halo, edge), (outer.at[0], 0, halo), (outer.at[1], edge, planes)):
        copies.append(pltpu.make_async_copy(piece, final.at[low:high], sems.at[len(copies)]))
        copies[-1].start()
    alone(ext, rate[...] * current[...])
    for first in range(0, planes, halo):
        here = pl.ds(first, halo)
        value = laplacian(ext, first + halo, *bands)
        value = 2.0 * current[here] - later[here] + value + injected[step, here]
        if first == 0 or first == edge:
            part[0 if first == 0 else 1] = value
        else:
            stage[pl.ds(first - halo, halo)] = value
    copies.append(pltpu.make_async_copy(stage, first_adjoint.at[halo:edge], sems.at[3]))
    copies[-1].start()
    for copy in copies:
        copy.wait()


def adjoint_outer_kernel(near, far, part, outer, sides):
    place_sides(sides, near, far)
    for side in range(2):
        outer[side] = part[side] + beyond(sides, side)


def write(moves, sems):
    copies = []
    for n, (piece, target, at, count) in enumerate(moves):
        copies.append(pltpu.make_async_copy(piece, target.at[pl.ds(at, count)], sems.at[n]))
        copies[n].start()
    for copy in copies:
        copy.wait()


def early_kernel(inner_kept, kept, outer, _, first_adjoint, total, sems):
    planes = total.shape[0]
    half = inner_kept.shape[0]
    moves = (
        (inner_kept, total, halo + core() * half, half),
        (kept, total, core() * (planes - halo), halo),
        (outer.at[0], first_adjoint, 0, halo),
        (outer.at[1], first_adjoint, planes - halo, halo),
    )
    write(moves, sems)


def finish_kernel(inner_got, got, _, total, sems):
    planes = total.shape[0]
    half = inner_got.shape[0]
    other = 1 - core()
    moves = (
        (inner_got, total, halo + other * half, half),
        (got, total, other * (planes - halo), halo),
    )
    write(moves, sems)


def swap(near_edge, far_edge):
    count = lax.axis_size("dom")
    near_pairs = [(i, i ^ 1) for i in range(count) if i ^ 1 < count]
    far_pairs = [(i, i + 1) for i in range(1, count - 1, 2)]
    far_pairs = far_pairs + [(b, a) for a, b in far_pairs]
    far = lax.ppermute(far_edge, "dom", far_pairs)
    return lax.ppermute(near_edge, "dom", near_pairs), far


def parts_kernel(keep, *refs):
    parts, total = refs[:-2], refs[-1]
    size = parts[0].shape[0]
    for n, part in enumerate(parts):
        here = pl.ds(n * size, size)
        total[here] = keep[here] + part[...]


def add_kernel(a, b, _, total):
    total[...] = a[...] + b[...]


def first_sum(keep, send, after, count):
    shots = lax.axis_size("shot")
    pairs = [(i, i ^ 1) for i in range(shots)]
    across = [(i, i ^ 2) for i in range(shots)]
    size = send.shape[0] // count
    got = [lax.ppermute(send[n * size : (n + 1) * size], "shot", pairs) for n in range(count)]
    (kept,) = call(
        parts_kernel,
        (keep, *got, after),
        [vmem] * (1 + count) + [wherever],
        [(jax.ShapeDtypeStruct(keep.shape, jnp.float32), vmem)],
    )
    return kept, lax.ppermute(kept, "shot", across)


def second_sum(kept, got, after):
    shots = lax.axis_size("shot")
    pairs = [(i, i ^ 1) for i in range(shots)]
    (kept,) = call(
        add_kernel,
        (kept, got, after),
        [vmem, vmem, wherever],
        [(jax.ShapeDtypeStruct(kept.shape, jnp.float32), vmem)],
    )
    return kept, lax.ppermute(kept, "shot", pairs)


def per_device(
    wave_before,
    wave_current,
    adjoint_far,
    adjoint_near,
    labels,
    table,
    source_index,
    wavelet,
    receiver_index,
    residual,
):
    planes, nz, ny = wave_current.shape[1:]
    steps = wavelet.shape[1]
    odd = lax.axis_index("dom") % 2
    u0, u1 = wave_before[0], wave_current[0]
    a6, a5 = adjoint_far[0], adjoint_near[0]
    u0, u1, a6, a5, labels = (
        pltpu.with_memory_space_constraint(x, pltpu.HBM) for x in (u0, u1, a6, a5, labels)
    )
    whole = f32(planes, nz, ny)
    block = (whole, vmem)
    edge = (f32(halo, nz, ny), vmem)
    inner = planes - 2 * halo
    quarter = (f32(inner // 2, nz, ny), vmem)
    pair = (f32(2, halo, nz, ny), vmem)
    ext = pltpu.VMEM((planes + 2 * halo, nz, ny), jnp.float32)
    within = pltpu.VMEM((inner, nz, ny), jnp.float32)

    near_at = jnp.where(odd == 1, 0, planes - halo)
    near_edge = lax.dynamic_slice_in_dim(wave_current[0], near_at, halo, axis=0)
    far_edge = lax.dynamic_slice_in_dim(wave_current[0], planes - halo - near_at, halo, axis=0)
    u_halo = swap(near_edge, far_edge)

    rate, near_edge, far_edge, *bands, a5, u1, u0, a6 = call(
        prepare_kernel,
        (table, labels, a5, u1, u0, a6),
        [vmem] + [hbm] * 5,
        [block, edge, edge]
        + [(jax.ShapeDtypeStruct((n, n), jnp.bfloat16), vmem) for n in (ny, halo * nz)]
        + [block] * 4,
        [pltpu.VMEM((planes, nz, ny), jnp.int32), pltpu.SemaphoreType.DMA((5,))],
    )
    a_halo = swap(near_edge, far_edge)

    (injected,) = call(
        receivers_kernel,
        (receiver_index[0].T, residual[0], rate),
        [vmem, vmem, wherever],
        [(f32(steps, planes, nz, ny), vmem)],
    )

    laps = []
    previous, current = u0, u1
    later, adjoint = a6, a5
    for n in range(steps - 1):
        upcoming, lap, near_edge, far_edge = call(
            functools.partial(forward_kernel, n),
            (*bands, source_index, wavelet, current, previous, *u_halo[::-1], rate, injected),
            [vmem] * 9 + [wherever],
            [block, block, edge, edge],
            [ext],
        )
        laps.append(lap)
        u_halo = swap(near_edge, far_edge)
        previous, current = current, upcoming
        step = steps - 1 - n
        if n < steps - 2:
            earlier, near_edge, far_edge = call(
                functools.partial(adjoint_kernel, step),
                (*bands, adjoint, later, *a_halo, rate, injected),
                [vmem] * 8,
                [block, edge, edge],
                [ext],
            )
        else:
            earlier, near_edge, far_edge, rest, part, keep, send, inner_wave = call(
                functools.partial(turn_kernel, steps - 1, step),
                (*bands, source_index, wavelet, adjoint, later, *a_halo, rate, injected, *laps,
                 current, previous, a5),
                [vmem] * 16,
                [block, edge, edge, pair, pair, quarter, quarter, (f32(inner, nz, ny), vmem)],
                [ext, ext, within],
            )
        if n < steps - 2:
            a_halo = swap(near_edge, far_edge)
        later, adjoint = adjoint, earlier

    inner_sum = first_sum(keep, send, keep, 4)
    near_edge, far_edge = call(
        pass_kernel,
        (near_edge, far_edge, inner_sum[0]),
        [vmem, vmem, wherever],
        [edge, edge],
    )
    a_halo = swap(near_edge, far_edge)
    outer = pltpu.VMEM((2, halo, nz, ny), jnp.float32)
    keep, send, outer_wave = call(
        forward_outer_kernel,
        (*u_halo[::-1], rate, part, rest, a5),
        [vmem] * 6,
        [edge, edge, pair],
        [outer, outer],
    )
    outer_sum = first_sum(keep, send, inner_sum[1], 2)
    first_adjoint, final, part = call(
        functools.partial(adjoint_inner_kernel, 0),
        (*bands, adjoint, later, rate, injected, inner_wave, outer_wave),
        [vmem] * 8,
        [(whole, hbm), (whole, hbm), pair],
        [ext, within, pltpu.SemaphoreType.DMA((4,))],
    )
    (last_outer,) = call(
        adjoint_outer_kernel,
        (*a_halo, part),
        [vmem] * 3,
        [pair],
        [outer],
        cost=2000000000,
    )
    inner_kept, inner_got = second_sum(*inner_sum, last_outer)
    kept, got = second_sum(*outer_sum, last_outer)
    first_adjoint, total = call(
        early_kernel,
        (inner_kept, kept, last_outer, first_adjoint),
        [vmem] * 3 + [hbm],
        [(whole, hbm), (whole, hbm)],
        [pltpu.SemaphoreType.DMA((4,))],
        {3: 0},
    )
    (total,) = call(
        finish_kernel,
        (inner_got, got, total),
        [vmem] * 2 + [hbm],
        [(whole, hbm)],
        [pltpu.SemaphoreType.DMA((2,))],
        {2: 0},
    )
    return (final[None], first_adjoint[None], total)


def solution(mesh):
    placed = (
        P("shot", "dom", None, None),
        P("shot", "dom", None, None),
        P("shot", "dom", None, None),
        P("shot", "dom", None, None),
        P("dom", None, None),
        P(),
        P("shot", None),
        P("shot", None),
        P("shot", None, None),
        P("shot", None, None),
    )
    return jax.shard_map(
        per_device,
        mesh=mesh,
        in_specs=placed,
        out_specs=(
            P("shot", "dom", None, None),
            P("shot", "dom", None, None),
            P("dom", None, None),
        ),
        check_vma=False,
    )
```

```python
import functools

import jax
import jax.numpy as jnp
from jax import lax
from jax.experimental import pallas as pl
from jax.experimental.pallas import tpu as pltpu
from jax.sharding import PartitionSpec as P

centre_coef = -205.0 / 72.0
side_coefs = (8.0 / 5.0, -1.0 / 5.0, 8.0 / 315.0, -1.0 / 560.0)
unit = 5040.0
side_units = (8064.0, -1008.0, 128.0, -9.0)
halo = 4

vmem = pl.BlockSpec(memory_space=pltpu.VMEM)
hbm = pl.BlockSpec(memory_space=pltpu.HBM)
wherever = pl.BlockSpec(memory_space=pl.ANY)


def call(kernel, args, in_specs, outs, scratch=(), aliases={}, limit=24, cost=1024):
    return pl.pallas_call(
        kernel,
        out_shape=[
            pltpu.VMEM(shape.shape, shape.dtype) if spec is vmem else shape for shape, spec in outs
        ],
        in_specs=in_specs,
        out_specs=[spec for _, spec in outs],
        scratch_shapes=list(scratch),
        input_output_aliases=aliases,
        compiler_params=pltpu.CompilerParams(vmem_limit_bytes=limit * 1024 * 1024),
        cost_estimate=pl.CostEstimate(flops=cost, bytes_accessed=1024, transcendentals=0),
    )(*args)


def f32(*shape):
    return jax.ShapeDtypeStruct(shape, jnp.float32)


def band(size, block):
    row = lax.broadcasted_iota(jnp.int32, (size, size), 0)
    col = lax.broadcasted_iota(jnp.int32, (size, size), 1)
    apart = jnp.abs(row - col)
    value = jnp.zeros((size, size), jnp.float32)
    for k in range(1, 5):
        value = jnp.where(apart == k, side_units[k - 1], value)
    if block != size:
        value = jnp.where(lax.div(row, block) == lax.div(col, block), value, 0.0)
    return value.astype(jnp.bfloat16)


def pieces(value):
    high = value.astype(jnp.bfloat16)
    rest = value - high.astype(jnp.float32)
    middle = rest.astype(jnp.bfloat16)
    low = (rest - middle.astype(jnp.float32)).astype(jnp.bfloat16)
    return high, middle, low


def dot(a, b):
    return lax.dot_general(a, b, (((1,), (0,)), ((), ())), preferred_element_type=jnp.float32)


def laplacian(field, at, along_y, along_z):
    _, nz, ny = field.shape
    along_y, along_z = along_y[...], along_z[...]
    centre = field[pl.ds(at, halo)]
    high, middle, low = pieces(centre.reshape(halo * nz, ny))
    across = dot(low, along_y) + dot(along_z, low)
    across = across + (dot(middle, along_y) + dot(along_z, middle))
    across = across + (dot(high, along_y) + dot(along_z, high))
    result = 3.0 * centre_coef * centre + across.reshape(halo, nz, ny) * (1.0 / unit)
    for k in range(1, 5):
        result = result + side_coefs[k - 1] * (
            field[pl.ds(at + k, halo)] + field[pl.ds(at - k, halo)]
        )
    return result


def beyond(sides, side):
    outside = sides[side]
    result = None
    for k in range(4, 0, -1):
        if side == 0:
            term = outside[halo - k : halo]
        else:
            term = outside[:k]
        term = side_coefs[k - 1] * term
        if k < halo:
            empty = jnp.zeros((halo - k,) + outside.shape[1:], jnp.float32)
            term = jnp.concatenate([term, empty] if side == 0 else [empty, term], axis=0)
        result = term if result is None else result + term
    return result


def core():
    return lax.axis_index("shot") % 2


def place(ext, near, far):
    planes = ext.shape[0] - 2 * halo
    odd = lax.axis_index("dom") % 2
    spot = jnp.where(odd == 1, 0, planes + halo)
    ext[pl.ds(spot, halo)] = near[...]
    ext[pl.ds(planes + halo - spot, halo)] = far[...]


def place_sides(sides, near, far):
    odd = lax.axis_index("dom") % 2
    sides[1 - odd] = near[...]
    sides[odd] = far[...]


def alone(ext, block):
    planes = block.shape[0]
    empty = jnp.zeros((halo,) + block.shape[1:], jnp.float32)
    ext[pl.ds(0, halo)] = empty
    ext[pl.ds(planes + halo, halo)] = empty
    ext[pl.ds(halo, planes)] = block


def edge_spots(planes):
    odd = lax.axis_index("dom") % 2
    near = jnp.where(odd == 1, 0, planes - halo)
    return near, planes - halo - near


def add_source(field, first, planes, source, value):
    count, _, ny = field.shape
    x = source[0, 0] - lax.axis_index("dom") * planes - first
    z = source[0, 1]
    y = source[0, 2]

    @pl.when((x >= 0) & (x < count))
    def _():
        base = pl.multiple_of(lax.div(z, 8) * 8, 8)
        rows = lax.broadcasted_iota(jnp.int32, (8, ny), 0)
        cols = lax.broadcasted_iota(jnp.int32, (8, ny), 1)
        hit = (rows == z - base) & (cols == y)
        tile = field[x, pl.ds(base, 8), :]
        field[x, pl.ds(base, 8), :] = tile + jnp.where(hit, value, 0.0)


def prepare_kernel(
    table, labels, near_field, *refs
):
    sources, refs = refs[:3], refs[3:]
    rate, near_edge, far_edge, along_y, along_z, field, *targets = refs[:9]
    label, sems = refs[9:]
    planes = labels.shape[0]
    first = pltpu.make_async_copy(labels, label, sems.at[0])
    second = pltpu.make_async_copy(near_field, field, sems.at[1])
    first.start()
    second.start()
    others = []
    for n in range(3):
        others.append(pltpu.make_async_copy(sources[n], targets[n], sems.at[2 + n]))
        others[n].start()
    _, nz, ny = labels.shape
    along_y[...] = band(ny, ny)
    along_z[...] = band(halo * nz, nz)
    first.wait()
    for part in range(planes // halo):
        here = pl.ds(part * halo, halo)
        known = label[here]
        value = jnp.zeros(known.shape, jnp.float32)
        for region in range(table.shape[0]):
            value = jnp.where(known == region, table[region], value)
        rate[here] = value
    second.wait()
    near, far = edge_spots(planes)
    near_edge[...] = rate[pl.ds(near, halo)] * field[pl.ds(near, halo)]
    far_edge[...] = rate[pl.ds(far, halo)] * field[pl.ds(far, halo)]
    for copy in others:
        copy.wait()


def receivers_kernel(index, values, _, injected):
    steps, planes, nz, ny = injected.shape
    count = index.shape[1]
    local = index[0:1, :] - lax.axis_index("dom") * planes
    cell = jnp.where((local >= 0) & (local < planes), local * nz + index[1:2, :], -1)
    at_y = lax.broadcasted_iota(jnp.int32, (ny, count), 0) == index[2:3, :]
    parts = []
    for step in range(steps):
        for piece in pieces(values[step : step + 1, :]):
            spread = jnp.where(at_y, piece.astype(jnp.float32), 0.0)
            parts.append(spread.astype(jnp.bfloat16))
    group = halo
    rows = group * nz
    for part in range(planes // group):
        at_cell = lax.broadcasted_iota(jnp.int32, (rows, count), 0) + part * rows == cell
        picked = jnp.where(at_cell, 1.0, 0.0).astype(jnp.bfloat16)
        for step in range(steps):
            total = None
            for piece in reversed(parts[3 * step : 3 * step + 3]):
                term = lax.dot_general(
                    picked, piece, (((1,), (1,)), ((), ())), preferred_element_type=jnp.float32
                )
                total = term if total is None else total + term
            injected[step, pl.ds(part * group, group)] = total.reshape(group, nz, ny)


def forward_kernel(step, *refs):
    *bands, source, wavelet = refs[:4]
    refs = refs[4:]
    current, previous, far, near, rate, _, upcoming, lap, near_edge, far_edge, ext = refs
    planes = current.shape[0]
    place(ext, near, far)
    ext[pl.ds(halo, planes)] = current[...]
    for first in range(0, planes, halo):
        here = pl.ds(first, halo)
        value = laplacian(ext, first + halo, *bands)
        lap[here] = value
        upcoming[here] = 2.0 * current[here] - previous[here] + rate[here] * value
    add_source(upcoming, 0, planes, source, wavelet[0, step])
    near_at, far_at = edge_spots(planes)
    near_edge[...] = upcoming[pl.ds(near_at, halo)]
    far_edge[...] = upcoming[pl.ds(far_at, halo)]


def adjoint_kernel(step, *refs):
    bands, refs = refs[:2], refs[2:]
    current, later, near, far, rate, injected, earlier, near_edge, far_edge, ext = refs
    planes = current.shape[0]
    place(ext, near, far)
    ext[pl.ds(halo, planes)] = rate[...] * current[...]
    for first in range(0, planes, halo):
        here = pl.ds(first, halo)
        value = laplacian(ext, first + halo, *bands)
        earlier[here] = 2.0 * current[here] - later[here] + value + injected[step, here]
    near_at, far_at = edge_spots(planes)
    near_edge[...] = rate[pl.ds(near_at, halo)] * earlier[pl.ds(near_at, halo)]
    far_edge[...] = rate[pl.ds(far_at, halo)] * earlier[pl.ds(far_at, halo)]


def ahead_kernel(step, *refs):
    (*bands, current, later, rate, injected, earlier, ext) = refs
    alone(ext, rate[...] * current[...])
    for first in range(0, current.shape[0], halo):
        here = pl.ds(first, halo)
        value = laplacian(ext, first + halo, *bands)
        earlier[here] = 2.0 * current[here] - later[here] + value + injected[step, here]


def turn_kernel(forward_step, *refs):
    *bands, source, wavelet = refs[:4]
    refs = refs[4:]
    (current, later, near, far, rate, known, lap1, lap2, lap3, wave, before, a5,
     earlier, near_edge, far_edge, rest, part, keep, send, inner, sides, wide, grad) = refs
    planes = current.shape[0]
    place_sides(sides, near, far)
    alone(wide, wave[...])
    for first in range(0, planes, halo):
        here = pl.ds(first, halo)
        value = known[here]
        if first == 0:
            value = value + beyond(sides, 0)
        elif first == planes - halo:
            value = value + beyond(sides, 1)
        earlier[here] = value
        partial = later[here] * lap3[here] + current[here] * lap2[here] + value * lap1[here]
        value = laplacian(wide, first + halo, *bands)
        partial = partial + a5[here] * value
        value = 2.0 * wave[here] - before[here] + rate[here] * value
        if first == 0 or first == planes - halo:
            side = 0 if first == 0 else 1
            rest[side] = partial
            part[side] = value
        else:
            within = pl.ds(first - halo, halo)
            inner[within] = value
            grad[within] = partial
    for side, first in enumerate((0, planes - halo)):
        add_source(part.at[side], first, planes, source, wavelet[0, forward_step])
    add_source(inner, halo, planes, source, wavelet[0, forward_step])
    near_at, far_at = edge_spots(planes)
    near_edge[...] = rate[pl.ds(near_at, halo)] * earlier[pl.ds(near_at, halo)]
    far_edge[...] = rate[pl.ds(far_at, halo)] * earlier[pl.ds(far_at, halo)]
    half = keep.shape[0]
    mine = core() * half
    keep[...] = grad[pl.ds(mine, half)]
    send[...] = grad[pl.ds(half - mine, half)]


def forward_outer_kernel(far, near, rate, part, rest, a5, keep, send, outer, sides, grad):
    planes = rate.shape[0]
    place_sides(sides, near, far)
    for side, first in enumerate((0, planes - halo)):
        here = pl.ds(first, halo)
        value = beyond(sides, side)
        outer[side] = part[side] + rate[here] * value
        grad[side] = rest[side] + a5[here] * value
    keep[...] = grad[core()]
    send[...] = grad[1 - core()]


def last_edges_kernel(step, *refs):
    (*bands, current, later, rate, injected, near, far, _,
     near_edge, far_edge, part, ext) = refs
    planes = current.shape[0]
    near_edge[...] = near[...]
    far_edge[...] = far[...]
    alone(ext, rate[...] * current[...])
    for side, first in enumerate((0, planes - halo)):
        here = pl.ds(first, halo)
        value = laplacian(ext, first + halo, *bands)
        part[side] = 2.0 * current[here] - later[here] + value + injected[step, here]


def adjoint_inner_kernel(step, *refs):
    (*bands, current, later, rate, injected, inner, outer,
     first_adjoint, final, token, scaled, stage, sems) = refs
    planes = current.shape[0]
    edge = planes - halo
    copies = []
    for piece, low, high in ((inner, halo, edge), (outer.at[0], 0, halo), (outer.at[1], edge, planes)):
        copies.append(pltpu.make_async_copy(piece, final.at[low:high], sems.at[len(copies)]))
        copies[-1].start()
    token[...] = jnp.zeros_like(token)
    scaled[...] = rate[...] * current[...]
    for first in range(halo, edge, halo):
        here = pl.ds(first, halo)
        value = laplacian(scaled, first, *bands)
        stage[pl.ds(first - halo, halo)] = (
            2.0 * current[here] - later[here] + value + injected[step, here]
        )
    copies.append(pltpu.make_async_copy(stage, first_adjoint.at[halo:edge], sems.at[3]))
    copies[-1].start()
    for copy in copies:
        copy.wait()


def adjoint_outer_kernel(near, far, part, _, outer, sides):
    place_sides(sides, near, far)
    for side in range(2):
        outer[side] = part[side] + beyond(sides, side)


def write(moves, sems):
    copies = []
    for n, (piece, target, at, count) in enumerate(moves):
        copies.append(pltpu.make_async_copy(piece, target.at[pl.ds(at, count)], sems.at[n]))
        copies[n].start()
    for copy in copies:
        copy.wait()


def early_kernel(inner_kept, kept, outer, _, first_adjoint, total, sems):
    planes = total.shape[0]
    half = inner_kept.shape[0]
    moves = (
        (inner_kept, total, halo + core() * half, half),
        (kept, total, core() * (planes - halo), halo),
        (outer.at[0], first_adjoint, 0, halo),
        (outer.at[1], first_adjoint, planes - halo, halo),
    )
    write(moves, sems)


def finish_kernel(inner_got, got, _, total, sems):
    planes = total.shape[0]
    half = inner_got.shape[0]
    other = 1 - core()
    moves = (
        (inner_got, total, halo + other * half, half),
        (got, total, other * (planes - halo), halo),
    )
    write(moves, sems)


def swap(near_edge, far_edge):
    count = lax.axis_size("dom")
    near_pairs = [(i, i ^ 1) for i in range(count) if i ^ 1 < count]
    far_pairs = [(i, i + 1) for i in range(1, count - 1, 2)]
    far_pairs = far_pairs + [(b, a) for a, b in far_pairs]
    far = lax.ppermute(far_edge, "dom", far_pairs)
    return lax.ppermute(near_edge, "dom", near_pairs), far


def parts_kernel(keep, *refs):
    parts, total = refs[:-2], refs[-1]
    size = parts[0].shape[0]
    for n, part in enumerate(parts):
        here = pl.ds(n * size, size)
        total[here] = keep[here] + part[...]


def add_kernel(a, b, _, total):
    total[...] = a[...] + b[...]


def first_sum(keep, send, after, count):
    shots = lax.axis_size("shot")
    pairs = [(i, i ^ 1) for i in range(shots)]
    across = [(i, i ^ 2) for i in range(shots)]
    size = send.shape[0] // count
    got = [lax.ppermute(send[n * size : (n + 1) * size], "shot", pairs) for n in range(count)]
    (kept,) = call(
        parts_kernel,
        (keep, *got, after),
        [vmem] * (1 + count) + [wherever],
        [(jax.ShapeDtypeStruct(keep.shape, jnp.float32), vmem)],
    )
    return kept, lax.ppermute(kept, "shot", across)


def second_sum(kept, got, after):
    shots = lax.axis_size("shot")
    pairs = [(i, i ^ 1) for i in range(shots)]
    (kept,) = call(
        add_kernel,
        (kept, got, after),
        [vmem, vmem, wherever],
        [(jax.ShapeDtypeStruct(kept.shape, jnp.float32), vmem)],
    )
    return kept, lax.ppermute(kept, "shot", pairs)


def per_device(
    wave_before,
    wave_current,
    adjoint_far,
    adjoint_near,
    labels,
    table,
    source_index,
    wavelet,
    receiver_index,
    residual,
):
    planes, nz, ny = wave_current.shape[1:]
    steps = wavelet.shape[1]
    odd = lax.axis_index("dom") % 2
    u0, u1 = wave_before[0], wave_current[0]
    a6, a5 = adjoint_far[0], adjoint_near[0]
    u0, u1, a6, a5, labels = (
        pltpu.with_memory_space_constraint(x, pltpu.HBM) for x in (u0, u1, a6, a5, labels)
    )
    whole = f32(planes, nz, ny)
    block = (whole, vmem)
    edge = (f32(halo, nz, ny), vmem)
    inner = planes - 2 * halo
    quarter = (f32(inner // 2, nz, ny), vmem)
    pair = (f32(2, halo, nz, ny), vmem)
    ext = pltpu.VMEM((planes + 2 * halo, nz, ny), jnp.float32)
    within = pltpu.VMEM((inner, nz, ny), jnp.float32)

    near_at = jnp.where(odd == 1, 0, planes - halo)
    near_edge = lax.dynamic_slice_in_dim(wave_current[0], near_at, halo, axis=0)
    far_edge = lax.dynamic_slice_in_dim(wave_current[0], planes - halo - near_at, halo, axis=0)
    u_halo = swap(near_edge, far_edge)

    rate, near_edge, far_edge, *bands, a5, u1, u0, a6 = call(
        prepare_kernel,
        (table, labels, a5, u1, u0, a6),
        [vmem] + [hbm] * 5,
        [block, edge, edge]
        + [(jax.ShapeDtypeStruct((n, n), jnp.bfloat16), vmem) for n in (ny, halo * nz)]
        + [block] * 4,
        [pltpu.VMEM((planes, nz, ny), jnp.int32), pltpu.SemaphoreType.DMA((5,))],
    )
    a_halo = swap(near_edge, far_edge)

    (injected,) = call(
        receivers_kernel,
        (receiver_index[0].T, residual[0], rate),
        [vmem, vmem, wherever],
        [(f32(steps, planes, nz, ny), vmem)],
    )

    outer = pltpu.VMEM((2, halo, nz, ny), jnp.float32)
    laps = []
    known = injected
    previous, current = u0, u1
    later, adjoint = a6, a5
    for n in range(steps - 1):
        if n == steps - 2:
            (known,) = call(
                functools.partial(ahead_kernel, 1),
                (*bands, adjoint, later, rate, injected),
                [vmem] * 6,
                [block],
                [ext],
            )
        upcoming, lap, near_edge, far_edge = call(
            functools.partial(forward_kernel, n),
            (*bands, source_index, wavelet, current, previous, *u_halo[::-1], rate, known),
            [vmem] * 9 + [wherever],
            [block, block, edge, edge],
            [ext],
        )
        laps.append(lap)
        u_halo = swap(near_edge, far_edge)
        previous, current = current, upcoming
        step = steps - 1 - n
        if n < steps - 2:
            earlier, near_edge, far_edge = call(
                functools.partial(adjoint_kernel, step),
                (*bands, adjoint, later, *a_halo, rate, injected),
                [vmem] * 8,
                [block, edge, edge],
                [ext],
            )
        else:
            earlier, near_edge, far_edge, rest, part, keep, send, inner_wave = call(
                functools.partial(turn_kernel, steps - 1),
                (*bands, source_index, wavelet, adjoint, later, *a_halo, rate, known, *laps,
                 current, previous, a5),
                [vmem] * 16,
                [block, edge, edge, pair, pair, quarter, quarter, (f32(inner, nz, ny), vmem)],
                [outer, ext, within],
            )
        if n < steps - 2:
            a_halo = swap(near_edge, far_edge)
        later, adjoint = adjoint, earlier

    inner_sum = first_sum(keep, send, keep, 4)
    near_edge, far_edge, last_part = call(
        functools.partial(last_edges_kernel, 0),
        (*bands, adjoint, later, rate, injected, near_edge, far_edge, inner_sum[0]),
        [vmem] * 8 + [wherever],
        [edge, edge, pair],
        [ext],
    )
    a_halo = swap(near_edge, far_edge)
    keep, send, outer_wave = call(
        forward_outer_kernel,
        (*u_halo[::-1], rate, part, rest, a5),
        [vmem] * 6,
        [edge, edge, pair],
        [outer, outer],
    )
    outer_sum = first_sum(keep, send, inner_sum[1], 2)
    first_adjoint, final, token = call(
        functools.partial(adjoint_inner_kernel, 0),
        (*bands, adjoint, later, rate, injected, inner_wave, outer_wave),
        [vmem] * 8,
        [(whole, hbm), (whole, hbm), (f32(8, 128), vmem)],
        [pltpu.VMEM((planes, nz, ny), jnp.float32), within, pltpu.SemaphoreType.DMA((4,))],
    )
    (last_outer,) = call(
        adjoint_outer_kernel,
        (*a_halo, last_part, token),
        [vmem] * 3 + [wherever],
        [pair],
        [outer],
        cost=2000000000,
    )
    inner_kept, inner_got = second_sum(*inner_sum, last_outer)
    kept, got = second_sum(*outer_sum, last_outer)
    first_adjoint, total = call(
        early_kernel,
        (inner_kept, kept, last_outer, first_adjoint),
        [vmem] * 3 + [hbm],
        [(whole, hbm), (whole, hbm)],
        [pltpu.SemaphoreType.DMA((4,))],
        {3: 0},
    )
    (total,) = call(
        finish_kernel,
        (inner_got, got, total),
        [vmem] * 2 + [hbm],
        [(whole, hbm)],
        [pltpu.SemaphoreType.DMA((2,))],
        {2: 0},
    )
    return (final[None], first_adjoint[None], total)


def solution(mesh):
    placed = (
        P("shot", "dom", None, None),
        P("shot", "dom", None, None),
        P("shot", "dom", None, None),
        P("shot", "dom", None, None),
        P("dom", None, None),
        P(),
        P("shot", None),
        P("shot", None),
        P("shot", None, None),
        P("shot", None, None),
    )
    return jax.shard_map(
        per_device,
        mesh=mesh,
        in_specs=placed,
        out_specs=(
            P("shot", "dom", None, None),
            P("shot", "dom", None, None),
            P("dom", None, None),
        ),
        check_vma=False,
    )
```
